128 devices in a mesh: dp: 8 (over z, x_lo), row: 4 (over x_hi, core), col: 4 (over y).
Axes of the slice: x: 4 (x_hi: 2, x_lo: 2; x = x_hi * 2 + x_lo), y: 4, z: 4, core: 2. Of those that a mesh axis runs over, the one named last changes fastest.
Arguments:
- stream_in: float32 [4096, 1024], P(('dp', 'col'), 'row'), may hold values from -6 to 6
- cotangent: float32 [4096, 1024], P(('dp', 'col'), 'row'), may hold values from -6 to 6
- mixer_gain: float32 [1024], P('row'), may hold values from 0.1 to 1.9
- mixer_input: bfloat16 [3, 1024, 1024], P(None, 'row', 'col'), may hold values from -0.1875 to 0.1875
- mixer_kernel: float32 [3, 1024], P(None, 'col'), may hold values from -3 to 3
- mixer_output: bfloat16 [1024, 1024], P('col', 'row'), may hold values from -0.1875 to 0.1875
- front_gain: float32 [1024], P('row'), may hold values from 0.1 to 1.9
- front_upper: bfloat16 [2, 1024, 4608], P(None, 'row', 'col'), may hold values from -0.1875 to 0.1875
- front_lower: bfloat16 [4608, 1024], P('col', 'row'), may hold values from -0.09375 to 0.09375
- attend_gain: float32 [1024], P('row'), may hold values from 0.1 to 1.9
- attend_query: bfloat16 [1024, 1024], P('row', 'col'), may hold values from -0.1875 to 0.1875
- attend_keyval: bfloat16 [2, 1024, 512], P(None, 'row', 'col'), may hold values from -0.1875 to 0.1875
- query_gain: float32 [64], replicated, may hold values from 0.6 to 1.4
- key_gain: float32 [64], replicated, may hold values from 0.6 to 1.4
- attend_output: bfloat16 [1024, 1024], P('col', 'row'), may hold values from -0.75 to 0.75
- rear_gain: float32 [1024], P('row'), may hold values from 0.1 to 1.9
- rear_upper: bfloat16 [2, 1024, 4608], P(None, 'row', 'col'), may hold values from -0.1875 to 0.1875
- rear_lower: bfloat16 [4608, 1024], P('col', 'row'), may hold values from -0.09375 to 0.09375
Outputs:
- block_out: float32 [4096, 1024], P(('dp', 'col'), 'row')
- grad_input: float32 [4096, 1024], P(('dp', 'col'), 'row')
- grad_mixer_gain: float32 [1024], P('row')
- grad_mixer_input: float32 [3, 1024, 1024], P(None, 'row', 'col')
- grad_mixer_kernel: float32 [3, 1024], P(None, 'col')
- grad_mixer_output: float32 [1024, 1024], P('col', 'row')
- grad_front_gain: float32 [1024], P('row')
- grad_front_upper: float32 [2, 1024, 4608], P(None, 'row', 'col')
- grad_front_lower: float32 [4608, 1024], P('col', 'row')
- grad_attend_gain: float32 [1024], P('row')
- grad_attend_query: float32 [1024, 1024], P('row', 'col')
- grad_attend_keyval: float32 [2, 1024, 512], P(None, 'row', 'col')
- grad_query_gain: float32 [64], replicated
- grad_key_gain: float32 [64], replicated
- grad_attend_output: float32 [1024, 1024], P('col', 'row')
- grad_rear_gain: float32 [1024], P('row')
- grad_rear_upper: float32 [2, 1024, 4608], P(None, 'row', 'col')
- grad_rear_lower: float32 [4608, 1024], P('col', 'row')
The draws below stay inside these ranges and needn't reach their ends.
All inputs are finite; a program needn't handle non-finite values.
Results may differ from the reference program's by a relative error of at most 0.022.
Values may be sent and summed in bfloat16 or wider, within the bound.
No kernel may reach another device: no remote copies, remote signals or barrier semaphores. Data moves between devices by JAX's collectives and lax.ppermute only.
A program may use at most 128 MiB of HBM per device.

```python
import jax
import jax.numpy as jnp
from jax import lax

D = 1024
FF = 4608
H = 16
KVH = 8
HD = 64
KW = 3
LEN = 128
TOKENS = 4096
N_DP = 8
N_ROW = 4


def block_levels(stream_key, dims, cuts, least, high):
    def one(axis_at, blocks):
        steps = jax.random.uniform(jax.random.fold_in(jax.random.fold_in(stream_key, 6), axis_at), (blocks,), jnp.float32, least / len(cuts), high / len(cuts))
        return jnp.repeat(jnp.exp(steps), dims[axis_at] // blocks).reshape((-1,) + (1,) * (len(dims) - axis_at - 1))

    level = one(*cuts[0])
    for cut in cuts[1:]:
        level = level * one(*cut)
    return level


def bell_draw(rng, dims, spread, bound, shards=(), kind=jnp.bfloat16):
    entries = jax.random.normal(rng, dims, jnp.float32) * spread
    if len(shards) > 0:
        entries = block_levels(rng, dims, shards, -0.22, 0.18) * entries
    return jnp.clip(entries, min=-bound, max=bound).astype(kind)


def setup_inputs(seed: int = 0) -> dict:
    splits = jax.random.split(jax.random.key(seed), 19)
    return {
        "stream_in": bell_draw(splits[0], (TOKENS, D), 1.0, 6.0, ((0, 32), (1, 4)), jnp.float32),
        "cotangent": bell_draw(splits[1], (TOKENS, D), 1.0, 6.0, ((0, 32), (1, 4)), jnp.float32),
        "mixer_gain": jnp.clip(1.0 + 0.18 * jax.random.normal(splits[2], (D,), jnp.float32), 0.1, 1.9),
        "mixer_input": bell_draw(splits[3], (3, D, D), D ** -0.5, 0.1875, ((1, 4), (2, 4))),
        "mixer_kernel": bell_draw(splits[4], (KW, D), 0.6, 3.0, ((1, 4),), jnp.float32),
        "mixer_output": bell_draw(splits[5], (D, D), D ** -0.5, 0.1875, ((0, 4), (1, 4))),
        "front_gain": jnp.clip(1.0 + 0.18 * jax.random.normal(splits[6], (D,), jnp.float32), 0.1, 1.9),
        "front_upper": bell_draw(splits[7], (2, D, FF), D ** -0.5, 0.1875, ((1, 4), (2, 4))),
        "front_lower": bell_draw(splits[8], (FF, D), FF ** -0.5, 0.09375, ((0, 4), (1, 4))),
        "attend_gain": jnp.clip(1.0 + 0.18 * jax.random.normal(splits[9], (D,), jnp.float32), 0.1, 1.9),
        "attend_query": bell_draw(splits[10], (D, H * HD), D ** -0.5, 0.1875, ((0, 4), (1, 4))),
        "attend_keyval": bell_draw(splits[11], (2, D, KVH * HD), D ** -0.5, 0.1875, ((1, 4), (2, 4))),
        "query_gain": jnp.clip(1.0 + 0.08 * jax.random.normal(splits[12], (HD,), jnp.float32), 0.6, 1.4),
        "key_gain": jnp.clip(1.0 + 0.08 * jax.random.normal(splits[13], (HD,), jnp.float32), 0.6, 1.4),
        "attend_output": bell_draw(splits[14], (H * HD, D), HD ** -0.5, 0.75, ((0, 4), (1, 4))),
        "rear_gain": jnp.clip(1.0 + 0.18 * jax.random.normal(splits[15], (D,), jnp.float32), 0.1, 1.9),
        "rear_upper": bell_draw(splits[16], (2, D, FF), D ** -0.5, 0.1875, ((1, 4), (2, 4))),
        "rear_lower": bell_draw(splits[17], (FF, D), FF ** -0.5, 0.09375, ((0, 4), (1, 4))),
    }


EPS = 1e-05
THETA = 1000000.0
MASKED = -1e+30

def matmul(left, right):
    return jnp.dot(left, right, preferred_element_type=jnp.float32)

def contract_rows(left, right):
    return lax.dot_general(left, right, (((0,), (0,)), ((), ())), preferred_element_type=jnp.float32)

def contract_cols(left, right):
    return lax.dot_general(left, right, (((1,), (1,)), ((), ())), preferred_element_type=jnp.float32)

def norm_forward(values, gain):
    scaling = lax.rsqrt(lax.optimization_barrier(jnp.mean(values * values, axis=-1, keepdims=True)) + EPS)
    normed = values * scaling
    return (normed, scaling, normed * gain)

def norm_backward(upstream, normed, scaling, gain):
    scaled_up = upstream * gain
    inner = lax.optimization_barrier(jnp.mean(scaled_up * normed, axis=-1, keepdims=True))
    return scaling * (scaled_up - normed * inner)

def rope_tables(length):
    half = HD // 2
    freqs = jnp.power(THETA, -(jnp.arange(half, dtype=jnp.float32) * 2.0 / HD))
    angles = jnp.arange(length, dtype=jnp.float32)[:, None] * freqs[None, :]
    cosine = jnp.concatenate([jnp.cos(angles), jnp.cos(angles)], axis=1)[:, None, :]
    sine = jnp.concatenate([jnp.sin(angles), jnp.sin(angles)], axis=1)[:, None, :]
    return (cosine, sine)

def rotate_half(values):
    half = values.shape[-1] // 2
    return jnp.concatenate([-values[..., half:], values[..., :half]], axis=-1)

def rotate_back(values):
    half = values.shape[-1] // 2
    return jnp.concatenate([values[..., half:], -values[..., :half]], axis=-1)

def attention_scores(turned_query, turned_keys):
    length = turned_query.shape[0]
    key_heads = turned_keys.shape[1]
    query_group = turned_query.reshape(length, key_heads, -1, HD)
    scores = jnp.einsum('qkgd,skd->kgqs', query_group.astype(jnp.float32), turned_keys.astype(jnp.float32)) * HD ** (-0.5)
    causal = jnp.arange(length)[:, None] >= jnp.arange(length)[None, :]
    return jnp.where(causal, scores, MASKED)

def attention_forward(projected, query_gain, key_gain, heads, key_heads):
    length = projected.shape[0]
    query = projected[:, :heads * HD].reshape(length, heads, HD)
    keys = projected[:, heads * HD:(heads + key_heads) * HD].reshape(length, key_heads, HD)
    values = projected[:, (heads + key_heads) * HD:].reshape(length, key_heads, HD).astype(jnp.bfloat16)
    query_hat, query_scale, query_normed = norm_forward(query, query_gain)
    keys_hat, keys_scale, keys_normed = norm_forward(keys, key_gain)
    cosine, sine = rope_tables(length)
    turned_query = (query_normed * cosine + rotate_half(query_normed) * sine).astype(jnp.bfloat16)
    turned_keys = (keys_normed * cosine + rotate_half(keys_normed) * sine).astype(jnp.bfloat16)
    scores = attention_scores(turned_query, turned_keys)
    peak = lax.optimization_barrier(jnp.max(scores, axis=-1, keepdims=True))
    logsum = peak + jnp.log(lax.optimization_barrier(jnp.sum(jnp.exp(scores - peak), axis=-1, keepdims=True)))
    probs = jnp.exp(scores - logsum).astype(jnp.bfloat16)
    mixed = jnp.einsum('kgqs,skd->qkgd', probs.astype(jnp.float32), values.astype(jnp.float32))
    output = mixed.reshape(length, heads * HD).astype(jnp.bfloat16)
    saved = (query_hat, query_scale, keys_hat, keys_scale, turned_query, turned_keys, values, logsum)
    return (output, saved)

def attention_backward(upstream, saved, query_gain, key_gain):
    query_hat, query_scale, keys_hat, keys_scale, turned_query, turned_keys, values, logsum = saved
    length = query_hat.shape[0]
    heads = query_hat.shape[1]
    key_heads = keys_hat.shape[1]
    upstream_b = upstream.astype(jnp.bfloat16).reshape(length, key_heads, heads // key_heads, HD)
    scores = attention_scores(turned_query, turned_keys)
    probs = jnp.exp(scores - logsum)
    probs_b = probs.astype(jnp.bfloat16)
    values_grad = jnp.einsum('kgqs,qkgd->skd', probs_b.astype(jnp.float32), upstream_b.astype(jnp.float32)).astype(jnp.bfloat16)
    probs_grad = jnp.einsum('qkgd,skd->kgqs', upstream_b.astype(jnp.float32), values.astype(jnp.float32))
    delta = lax.optimization_barrier(jnp.sum(probs * probs_grad, axis=-1, keepdims=True))
    scores_grad = (probs * (probs_grad - delta)).astype(jnp.bfloat16)
    query_group = turned_query.reshape(length, key_heads, heads // key_heads, HD)
    query_back = jnp.einsum('kgqs,skd->qkgd', scores_grad.astype(jnp.float32), turned_keys.astype(jnp.float32)).reshape(length, heads, HD) * HD ** (-0.5)
    keys_back = jnp.einsum('kgqs,qkgd->skd', scores_grad.astype(jnp.float32), query_group.astype(jnp.float32)) * HD ** (-0.5)
    cosine, sine = rope_tables(length)
    query_unspun = query_back * cosine + rotate_back(query_back * sine)
    keys_unspun = keys_back * cosine + rotate_back(keys_back * sine)
    query_grad = norm_backward(query_unspun, query_hat, query_scale, query_gain).astype(jnp.bfloat16)
    keys_grad = norm_backward(keys_unspun, keys_hat, keys_scale, key_gain).astype(jnp.bfloat16)
    qgain_grad = lax.optimization_barrier(jnp.sum(query_unspun * query_hat, axis=(0, 1)))
    kgain_grad = lax.optimization_barrier(jnp.sum(keys_unspun * keys_hat, axis=(0, 1)))
    pieces = jnp.concatenate([query_grad.reshape(length, -1), keys_grad.reshape(length, -1), values_grad.reshape(length, -1)], axis=1)
    return (pieces, qgain_grad, kgain_grad)

def conv_forward(projected, kernel):
    width = kernel.shape[1]
    length = projected.shape[0]
    gate_in = projected[:, :width]
    gate_out = projected[:, width:2 * width]
    signal = projected[:, 2 * width:]
    padded = jnp.pad(gate_in * signal, ((KW - 1, 0), (0, 0)))
    convolved = padded[0:length] * kernel[0]
    for offset in range(1, KW):
        convolved = convolved + padded[offset:offset + length] * kernel[offset]
    return ((gate_out * convolved).astype(jnp.bfloat16), convolved, padded)

def conv_backward(upstream, projected, convolved, padded, kernel):
    width = kernel.shape[1]
    length = projected.shape[0]
    gate_in = projected[:, :width]
    gate_out = projected[:, width:2 * width]
    signal = projected[:, 2 * width:]
    gate_grad = upstream * convolved
    conv_grad = upstream * gate_out
    padded_grad = jnp.pad(conv_grad, ((0, KW - 1), (0, 0)))
    kernel_grad = jnp.stack([lax.optimization_barrier(jnp.sum(conv_grad * padded[offset:offset + length], axis=0)) for offset in range(KW)])
    mixed_grad = padded_grad[KW - 1:KW - 1 + length] * kernel[0]
    for offset in range(1, KW):
        mixed_grad = mixed_grad + padded_grad[KW - 1 - offset:KW - 1 - offset + length] * kernel[offset]
    pieces = jnp.concatenate([mixed_grad * signal, gate_grad, mixed_grad * gate_in], axis=1).astype(jnp.bfloat16)
    return (pieces, kernel_grad)

def ffn_forward(residual, gain, upper, lower):
    normed, scaling, inputs = norm_forward(residual, gain)
    inputs = inputs.astype(jnp.bfloat16)
    gating = matmul(inputs, upper[0])
    upward = matmul(inputs, upper[1])
    hidden = (jax.nn.silu(gating) * upward).astype(jnp.bfloat16)
    return (residual + matmul(hidden, lower), (normed, scaling, inputs, gating, upward, hidden))

def ffn_backward(upstream, saved, gain, upper, lower):
    normed, scaling, inputs, gating, upward, hidden = saved
    upstream_b = upstream.astype(jnp.bfloat16)
    lower_grad = contract_rows(hidden, upstream_b)
    hidden_grad = contract_cols(upstream_b, lower)
    sigmoid = jax.nn.sigmoid(gating)
    gating_grad = (hidden_grad * upward * sigmoid * (1.0 + gating * (1.0 - sigmoid))).astype(jnp.bfloat16)
    upward_grad = (hidden_grad * gating * sigmoid).astype(jnp.bfloat16)
    upper_grad = jnp.stack([contract_rows(inputs, gating_grad), contract_rows(inputs, upward_grad)])
    normed_grad = contract_cols(gating_grad, upper[0]) + contract_cols(upward_grad, upper[1])
    residual_grad = upstream + norm_backward(normed_grad, normed, scaling, gain)
    gain_grad = lax.optimization_barrier(jnp.sum(normed_grad * normed, axis=0))
    return (residual_grad, upper_grad, lower_grad, gain_grad)

def block_pass(stream, upstream, weights):
    mixer_gain, mixer_input, mixer_kernel, mixer_output, front_gain, front_upper, front_lower, attend_gain, attend_query, attend_keyval, query_gain, key_gain, attend_output, rear_gain, rear_upper, rear_lower = weights
    seqs = stream.shape[0] // LEN
    normed_one, scaling_one, inputs_one = norm_forward(stream, mixer_gain)
    inputs_one = inputs_one.astype(jnp.bfloat16)
    projected = jnp.concatenate([matmul(inputs_one, mixer_input[member]) for member in range(3)], axis=1)
    mixes, convolved, padded = jax.vmap(conv_forward, in_axes=(0, None))(projected.reshape(seqs, LEN, -1), mixer_kernel)
    mixes = mixes.reshape(-1, D)
    first = stream + matmul(mixes, mixer_output)
    second, front_saved = ffn_forward(first, front_gain, front_upper, front_lower)
    normed_three, scaling_three, inputs_three = norm_forward(second, attend_gain)
    inputs_three = inputs_three.astype(jnp.bfloat16)
    projected_three = jnp.concatenate([matmul(inputs_three, attend_query), matmul(inputs_three, attend_keyval[0]), matmul(inputs_three, attend_keyval[1])], axis=1)
    attended, attn_saved = lax.map(lambda rows: attention_forward(rows, query_gain, key_gain, H, KVH), projected_three.reshape(seqs, LEN, -1))
    attended = attended.reshape(-1, H * HD)
    third = second + matmul(attended, attend_output)
    fourth, rear_saved = ffn_forward(third, rear_gain, rear_upper, rear_lower)
    third_grad, rear_upper_grad, rear_lower_grad, rear_gain_grad = ffn_backward(upstream, rear_saved, rear_gain, rear_upper, rear_lower)
    third_b = third_grad.astype(jnp.bfloat16)
    attend_output_grad = contract_rows(attended, third_b)
    attended_grad = contract_cols(third_b, attend_output)
    pieces, qgain_grads, kgain_grads = lax.map(lambda packed: attention_backward(packed[0], packed[1], query_gain, key_gain), (attended_grad.reshape(seqs, LEN, -1), attn_saved))
    pieces = pieces.reshape(-1, pieces.shape[-1])
    query_width = H * HD
    key_width = KVH * HD
    query_piece = pieces[:, :query_width]
    keys_piece = pieces[:, query_width:query_width + key_width]
    values_piece = pieces[:, query_width + key_width:]
    attend_query_grad = contract_rows(inputs_three, query_piece)
    keyval_grad = jnp.stack([contract_rows(inputs_three, keys_piece), contract_rows(inputs_three, values_piece)])
    normed_three_grad = contract_cols(query_piece, attend_query) + contract_cols(keys_piece, attend_keyval[0]) + contract_cols(values_piece, attend_keyval[1])
    second_grad = third_grad + norm_backward(normed_three_grad, normed_three, scaling_three, attend_gain)
    attend_gain_grad = lax.optimization_barrier(jnp.sum(normed_three_grad * normed_three, axis=0))
    first_grad, front_upper_grad, front_lower_grad, front_gain_grad = ffn_backward(second_grad, front_saved, front_gain, front_upper, front_lower)
    first_b = first_grad.astype(jnp.bfloat16)
    mixer_output_grad = contract_rows(mixes, first_b)
    mixes_grad = contract_cols(first_b, mixer_output)
    conv_pieces, kernel_grads = jax.vmap(conv_backward, in_axes=(0, 0, 0, 0, None))(mixes_grad.reshape(seqs, LEN, D), projected.reshape(seqs, LEN, -1), convolved, padded, mixer_kernel)
    conv_pieces = conv_pieces.reshape(-1, 3 * D)
    mixer_kernel_grad = lax.optimization_barrier(jnp.sum(kernel_grads, axis=0))
    mixer_input_grad = jnp.stack([contract_rows(inputs_one, conv_pieces[:, member * D:(member + 1) * D]) for member in range(3)])
    normed_one_grad = contract_cols(conv_pieces[:, 0:D], mixer_input[0])
    for member in range(1, 3):
        normed_one_grad = normed_one_grad + contract_cols(conv_pieces[:, member * D:(member + 1) * D], mixer_input[member])
    stream_grad = first_grad + norm_backward(normed_one_grad, normed_one, scaling_one, mixer_gain)
    mixer_gain_grad = lax.optimization_barrier(jnp.sum(normed_one_grad * normed_one, axis=0))
    grads = (mixer_gain_grad, mixer_input_grad, mixer_kernel_grad, mixer_output_grad, front_gain_grad, front_upper_grad, front_lower_grad, attend_gain_grad, attend_query_grad, keyval_grad, lax.optimization_barrier(jnp.sum(qgain_grads, axis=0)), lax.optimization_barrier(jnp.sum(kgain_grads, axis=0)), attend_output_grad, rear_gain_grad, rear_upper_grad, rear_lower_grad)
    return ((fourth, stream_grad), grads)

def reference(stream_in, cotangent, mixer_gain, mixer_input, mixer_kernel, mixer_output, front_gain, front_upper, front_lower, attend_gain, attend_query, attend_keyval, query_gain, key_gain, attend_output, rear_gain, rear_upper, rear_lower):
    weights = (mixer_gain, mixer_input, mixer_kernel, mixer_output, front_gain, front_upper, front_lower, attend_gain, attend_query, attend_keyval, query_gain, key_gain, attend_output, rear_gain, rear_upper, rear_lower)
    block = N_ROW * LEN

    def step(carry, packed):
        outputs, grads = block_pass(packed[0], packed[1], weights)
        return (tuple((running + update for running, update in zip(carry, grads))), outputs)
    start = tuple((jnp.zeros(weight.shape, jnp.float32) for weight in weights))
    totals, outputs = lax.scan(step, start, (stream_in.reshape(N_DP, block, D), cotangent.reshape(N_DP, block, D)))
    block_out = outputs[0].reshape(TOKENS, D)
    grad_input = outputs[1].reshape(TOKENS, D)
    return (block_out, grad_input, totals[0], totals[1], totals[2], totals[3], totals[4], totals[5], totals[6], totals[7], totals[8], totals[9], totals[10], totals[11], totals[12], totals[13], totals[14], totals[15])
```

```python
import jax
import jax.numpy as jnp
from jax import lax
from jax.sharding import Mesh
from jax.sharding import PartitionSpec as P

D = 1024
HD = 64
KW = 3


EPS = 1e-05
THETA = 1000000.0
MASKED = -1e30

def contract_rows(left, right):
    return lax.dot_general(
        left, right, (((0,), (0,)), ((), ())), preferred_element_type=jnp.float32
    )


def contract_cols(left, right):
    return lax.dot_general(
        left, right, (((1,), (1,)), ((), ())), preferred_element_type=jnp.float32
    )


def head_norm(values, gain):
    scaling = lax.rsqrt(jnp.mean(values * values, axis=-1, keepdims=True) + EPS)
    normed = values * scaling
    return (normed, scaling, normed * gain)


def head_back(upstream, normed, scaling, gain):
    scaled_up = upstream * gain
    inner = jnp.mean(scaled_up * normed, axis=-1, keepdims=True)
    return scaling * (scaled_up - normed * inner)


def rope_tables(length):
    half = HD // 2
    freqs = jnp.power(THETA, -(jnp.arange(half, dtype=jnp.float32) * 2.0 / HD))
    angles = jnp.arange(length, dtype=jnp.float32)[:, None] * freqs[None, :]
    cosine = jnp.concatenate([jnp.cos(angles), jnp.cos(angles)], axis=1)[:, None, :]
    sine = jnp.concatenate([jnp.sin(angles), jnp.sin(angles)], axis=1)[:, None, :]
    return (cosine, sine)


def rotate_half(values):
    half = values.shape[-1] // 2
    return jnp.concatenate([-values[..., half:], values[..., :half]], axis=-1)


def rotate_back(values):
    half = values.shape[-1] // 2
    return jnp.concatenate([values[..., half:], -values[..., :half]], axis=-1)


def attention_scores(turned_query, turned_keys):
    length = turned_query.shape[0]
    key_heads = turned_keys.shape[1]
    query_group = turned_query.reshape(length, key_heads, -1, HD)
    scores = jnp.einsum(
        "qkgd,skd->kgqs", query_group, turned_keys, preferred_element_type=jnp.float32
    ) * HD ** (-0.5)
    causal = jnp.arange(length)[:, None] >= jnp.arange(length)[None, :]
    return jnp.where(causal, scores, MASKED)


def attention_forward(projected, query_gain, key_gain, heads, key_heads):
    length = projected.shape[0]
    query = projected[:, : heads * HD].reshape(length, heads, HD)
    keys = projected[:, heads * HD : (heads + key_heads) * HD].reshape(length, key_heads, HD)
    values = (
        projected[:, (heads + key_heads) * HD :].reshape(length, key_heads, HD).astype(jnp.bfloat16)
    )
    query_hat, query_scale, query_normed = head_norm(query, query_gain)
    keys_hat, keys_scale, keys_normed = head_norm(keys, key_gain)
    cosine, sine = rope_tables(length)
    turned_query = (query_normed * cosine + rotate_half(query_normed) * sine).astype(jnp.bfloat16)
    turned_keys = (keys_normed * cosine + rotate_half(keys_normed) * sine).astype(jnp.bfloat16)
    scores = attention_scores(turned_query, turned_keys)
    peak = jnp.max(scores, axis=-1, keepdims=True)
    logsum = peak + jnp.log(jnp.sum(jnp.exp(scores - peak), axis=-1, keepdims=True))
    probs = jnp.exp(scores - logsum).astype(jnp.bfloat16)
    mixed = jnp.einsum("kgqs,skd->qkgd", probs, values, preferred_element_type=jnp.float32)
    output = mixed.reshape(length, heads * HD).astype(jnp.bfloat16)
    saved = (
        query_hat,
        query_scale,
        keys_hat,
        keys_scale,
        turned_query,
        turned_keys,
        values,
        logsum,
    )
    return (output, saved)


def attention_backward(upstream, saved, query_gain, key_gain):
    query_hat, query_scale, keys_hat, keys_scale, turned_query, turned_keys, values, logsum = saved
    length = query_hat.shape[0]
    heads = query_hat.shape[1]
    key_heads = keys_hat.shape[1]
    upstream_b = upstream.astype(jnp.bfloat16).reshape(length, key_heads, heads // key_heads, HD)
    scores = attention_scores(turned_query, turned_keys)
    probs = jnp.exp(scores - logsum)
    probs_b = probs.astype(jnp.bfloat16)
    values_grad = jnp.einsum(
        "kgqs,qkgd->skd", probs_b, upstream_b, preferred_element_type=jnp.float32
    ).astype(jnp.bfloat16)
    probs_grad = jnp.einsum(
        "qkgd,skd->kgqs", upstream_b, values, preferred_element_type=jnp.float32
    )
    delta = jnp.sum(probs * probs_grad, axis=-1, keepdims=True)
    scores_grad = (probs * (probs_grad - delta)).astype(jnp.bfloat16)
    query_group = turned_query.reshape(length, key_heads, heads // key_heads, HD)
    query_back = jnp.einsum(
        "kgqs,skd->qkgd", scores_grad, turned_keys, preferred_element_type=jnp.float32
    ).reshape(length, heads, HD) * HD ** (-0.5)
    keys_back = jnp.einsum(
        "kgqs,qkgd->skd", scores_grad, query_group, preferred_element_type=jnp.float32
    ) * HD ** (-0.5)
    cosine, sine = rope_tables(length)
    query_unspun = query_back * cosine + rotate_back(query_back * sine)
    keys_unspun = keys_back * cosine + rotate_back(keys_back * sine)
    query_grad = head_back(query_unspun, query_hat, query_scale, query_gain).astype(jnp.bfloat16)
    keys_grad = head_back(keys_unspun, keys_hat, keys_scale, key_gain).astype(jnp.bfloat16)
    qgain_grad = jnp.sum(query_unspun * query_hat, axis=(0, 1))
    kgain_grad = jnp.sum(keys_unspun * keys_hat, axis=(0, 1))
    pieces = jnp.concatenate(
        [
            query_grad.reshape(length, -1),
            keys_grad.reshape(length, -1),
            values_grad.reshape(length, -1),
        ],
        axis=1,
    )
    return (pieces, qgain_grad, kgain_grad)


def conv_forward(projected, kernel):
    width = kernel.shape[1]
    length = projected.shape[0]
    gate_in = projected[:, :width]
    gate_out = projected[:, width : 2 * width]
    signal = projected[:, 2 * width :]
    padded = jnp.pad(gate_in * signal, ((KW - 1, 0), (0, 0)))
    convolved = padded[0:length] * kernel[0]
    for offset in range(1, KW):
        convolved = convolved + padded[offset : offset + length] * kernel[offset]
    return ((gate_out * convolved).astype(jnp.bfloat16), convolved, padded)


def conv_backward(upstream, projected, convolved, padded, kernel):
    width = kernel.shape[1]
    length = projected.shape[0]
    gate_in = projected[:, :width]
    gate_out = projected[:, width : 2 * width]
    signal = projected[:, 2 * width :]
    gate_grad = upstream * convolved
    conv_grad = upstream * gate_out
    padded_grad = jnp.pad(conv_grad, ((0, KW - 1), (0, 0)))
    kernel_grad = jnp.stack(
        [jnp.sum(conv_grad * padded[offset : offset + length], axis=0) for offset in range(KW)]
    )
    mixed_grad = padded_grad[KW - 1 : KW - 1 + length] * kernel[0]
    for offset in range(1, KW):
        mixed_grad = (
            mixed_grad + padded_grad[KW - 1 - offset : KW - 1 - offset + length] * kernel[offset]
        )
    pieces = jnp.concatenate([mixed_grad * signal, gate_grad, mixed_grad * gate_in], axis=1).astype(
        jnp.bfloat16
    )
    return (pieces, kernel_grad)


BF = jnp.bfloat16
F32 = jnp.float32


def xor_pairs(count, bits):
    return [(i, i ^ bits) for i in range(count)]


def from_core(x):
    return lax.ppermute(x, "core", xor_pairs(2, 1))


def from_facing(x):
    return lax.ppermute(x, ("xl", "xh"), xor_pairs(4, 3))


def from_xl(x):
    return lax.ppermute(x, "xl", xor_pairs(2, 1))


def from_z(x, bits):
    return lax.ppermute(x, "z", xor_pairs(4, bits))


def from_y(x, bits):
    return lax.ppermute(x, "y", xor_pairs(4, bits))


def gathered(shard):
    facing = from_facing(shard)
    return [shard, from_core(shard), facing, from_core(facing)]


def summed_y(x):
    sent = x.astype(BF)
    total = x
    for bits in (1, 3, 2):
        total = total + from_y(sent, bits).astype(F32)
    return total


def blocks(x):
    width = x.shape[1] // 4
    return [x[:, i * width : (i + 1) * width] for i in range(4)]


def xor_order(parts, index):
    low = (index & 1) == 1
    high = (index & 2) == 2
    a = [jnp.where(low, parts[i ^ 1], parts[i]) for i in range(4)]
    return [jnp.where(high, a[i ^ 2], a[i]) for i in range(4)]


def place():
    row = lax.axis_index("xh") * 2 + lax.axis_index("core")
    return row, lax.axis_index("y")


def spread_in(x):
    row, col = place()
    parts = []
    for bits in range(4):
        pairs = [(w * 4 + s, s * 4 + (w ^ bits)) for w in range(4) for s in range(4)]
        parts.append(lax.ppermute(x, ("xh", "core", "y"), pairs))
    return jnp.concatenate(xor_order(parts, row ^ col), axis=1)


def bring_back(x):
    row, col = place()
    parts = xor_order(blocks(x.astype(BF)), row ^ col)
    total = None
    for bits in range(4):
        pairs = [(s * 4 + c, (c ^ bits) * 4 + s) for s in range(4) for c in range(4)]
        got = lax.ppermute(parts[bits], ("xh", "core", "y"), pairs).astype(F32)
        total = got if total is None else total + got
    return total


def dp_sum(g):
    z = lax.axis_index("z")
    xl = lax.axis_index("xl")
    g = g.astype(BF)
    quarter = g.shape[0] // 4
    half = quarter // 2

    def chunk(at):
        return lax.dynamic_slice_in_dim(g, at * quarter, quarter, 0)

    total = chunk(z).astype(F32)
    for bits in (1, 3, 2):
        total = total + from_z(chunk(z ^ bits), bits).astype(F32)
    sent = lax.dynamic_slice_in_dim(total.astype(BF), (1 - xl) * half, half, 0)
    kept = lax.dynamic_slice_in_dim(total, xl * half, half, 0)
    mine = (kept + from_xl(sent).astype(F32)).astype(BF)
    other = from_xl(mine)
    first = jnp.where(xl == 0, mine, other)
    second = jnp.where(xl == 0, other, mine)
    piece = jnp.concatenate([first, second], axis=0)
    pieces = [piece] + [from_z(piece, bits) for bits in (1, 2, 3)]
    return jnp.concatenate(xor_order(pieces, z), axis=0).astype(F32)


def norm_forward(values, gain):
    scaling = lax.rsqrt(jnp.mean(values * values, axis=1, keepdims=True) + EPS)
    normed = values * scaling
    return (normed, scaling, (normed * gain).astype(BF))


def norm_backward(upstream, normed, scaling, gain):
    scaled_up = upstream * gain
    inner = jnp.mean(scaled_up * normed, axis=1, keepdims=True)
    return scaling * (scaled_up - normed * inner)


def dot(left, right):
    return jnp.dot(left, right, preferred_element_type=F32)


def up(inputs, weights):
    total = None
    for piece, weight in zip(blocks(inputs), weights):
        term = dot(piece, weight)
        total = term if total is None else total + term
    return total


def up_back(upstreams, weight_lists):
    outs = []
    for at in range(4):
        total = None
        for upstream, weights in zip(upstreams, weight_lists):
            term = contract_cols(upstream, weights[at])
            total = term if total is None else total + term
        outs.append(total)
    return jnp.concatenate(outs, axis=1)


def down(hidden, weights):
    return jnp.concatenate([dot(hidden, weight) for weight in weights], axis=1)


def down_back(upstream, weights):
    total = None
    for piece, weight in zip(blocks(upstream), weights):
        term = contract_cols(piece, weight)
        total = term if total is None else total + term
    return total


def four_wide(x):
    facing = from_facing(x)
    return jnp.concatenate([x, from_core(x), facing, from_core(facing)], axis=0)


def four_own(x):
    parts = blocks(x)
    facing = from_facing(jnp.concatenate(parts[2:], axis=1))
    width = parts[0].shape[1]
    return jnp.concatenate(
        [parts[0], from_core(parts[1]), facing[:, :width], from_core(facing[:, width:])], axis=0
    )


def ffn_forward(residual, gain, upper, lower):
    normed, scaling, inputs = norm_forward(residual, gain)
    gating = up(inputs, upper[0])
    upward = up(inputs, upper[1])
    hidden = (jax.nn.silu(gating) * upward).astype(BF)
    return down(hidden, lower), (normed, scaling, inputs, gating, upward, hidden)


def ffn_backward(upstream, saved, gain, upper, lower):
    normed, scaling, inputs, gating, upward, hidden = saved
    cb = upstream.astype(BF)
    hidden_grad = down_back(cb, lower)
    sigmoid = jax.nn.sigmoid(gating)
    gating_grad = (hidden_grad * upward * sigmoid * (1.0 + gating * (1.0 - sigmoid))).astype(BF)
    upward_grad = (hidden_grad * gating * sigmoid).astype(BF)
    normed_grad = up_back([gating_grad, upward_grad], upper)
    gain_grad = jnp.sum(normed_grad * normed, axis=0)
    lower_grad = contract_rows(four_wide(hidden), four_own(cb))
    pieces = jnp.concatenate([gating_grad, upward_grad], axis=1)
    upper_grad = contract_rows(four_own(inputs), four_wide(pieces))
    return norm_backward(normed_grad, normed, scaling, gain), upper_grad, lower_grad, gain_grad


def split_cols(x, count):
    width = x.shape[1] // count
    return jnp.concatenate([x[:, i * width : (i + 1) * width] for i in range(count)], axis=0)


def body(
    stream_in,
    cotangent,
    mixer_gain,
    mixer_input,
    mixer_kernel,
    mixer_output,
    front_gain,
    front_upper,
    front_lower,
    attend_gain,
    attend_query,
    attend_keyval,
    query_gain,
    key_gain,
    attend_output,
    rear_gain,
    rear_upper,
    rear_lower,
):
    gains = jnp.stack([mixer_gain, front_gain, attend_gain, rear_gain])
    gains = jnp.concatenate(gathered(gains), axis=1)
    x = spread_in(stream_in.astype(BF)).astype(F32)
    mi = gathered(mixer_input)
    mo = gathered(mixer_output)
    fu = gathered(front_upper)
    fl = gathered(front_lower)
    aq = gathered(attend_query)
    akv = gathered(attend_keyval)
    ao = gathered(attend_output)
    ru = gathered(rear_upper)
    rl = gathered(rear_lower)
    cot = spread_in(cotangent.astype(BF)).astype(F32)

    def member(lists, at):
        return [w[at] for w in lists]

    fu = [member(fu, 0), member(fu, 1)]
    ru = [member(ru, 0), member(ru, 1)]
    mi = [member(mi, 0), member(mi, 1), member(mi, 2)]
    akv = [member(akv, 0), member(akv, 1)]

    normed_one, scaling_one, inputs_one = norm_forward(x, gains[0])
    projected = jnp.concatenate([up(inputs_one, w) for w in mi], axis=1)
    mixes, convolved, padded = conv_forward(projected, mixer_kernel)
    first = x + summed_y(down(mixes, mo))
    partial, front_saved = ffn_forward(first, gains[1], fu, fl)
    second = first + summed_y(partial)
    normed_three, scaling_three, inputs_three = norm_forward(second, gains[2])
    projected_three = jnp.concatenate([up(inputs_three, w) for w in [aq] + akv], axis=1)
    heads = attend_query.shape[1] // HD
    key_heads = attend_keyval.shape[2] // HD
    attended, attn_saved = attention_forward(
        projected_three, query_gain, key_gain, heads, key_heads
    )
    third = second + summed_y(down(attended, ao))
    partial, rear_saved = ffn_forward(third, gains[3], ru, rl)
    fourth = stream_in + bring_back(partial + 0.25 * (third - x))

    back, rear_upper_grad, rear_lower_grad, rear_gain_grad = ffn_backward(
        cot, rear_saved, gains[3], ru, rl
    )
    rear_upper_grad = dp_sum(split_cols(rear_upper_grad, 2))
    rear_lower_grad = dp_sum(rear_lower_grad)
    third_grad = cot + summed_y(back)
    ab = third_grad.astype(BF)
    attended_grad = down_back(ab, ao)
    attend_output_grad = contract_rows(four_wide(attended), four_own(ab))
    pieces, qgain_grad, kgain_grad = attention_backward(
        attended_grad, attn_saved, query_gain, key_gain
    )
    bounds = [0, heads * HD, (heads + key_heads) * HD, (heads + 2 * key_heads) * HD]
    normed_three_grad = up_back(
        [pieces[:, bounds[i] : bounds[i + 1]] for i in range(3)], [aq] + akv
    )
    attend_gain_grad = jnp.sum(normed_three_grad * normed_three, axis=0)
    second_grad = third_grad + summed_y(
        norm_backward(normed_three_grad, normed_three, scaling_three, gains[2])
    )
    attn_grad = contract_rows(four_own(inputs_three), four_wide(pieces))
    attn_all = dp_sum(jnp.concatenate([split_cols(attn_grad, 2), attend_output_grad], axis=0))
    rows = attend_query.shape[0]
    attend_query_grad = attn_all[:rows]
    keyval_grad = jnp.stack(jnp.split(attn_all[rows : 2 * rows], 2, axis=1))
    attend_output_grad = attn_all[2 * rows :]

    back, front_upper_grad, front_lower_grad, front_gain_grad = ffn_backward(
        second_grad, front_saved, gains[1], fu, fl
    )
    front_upper_grad = dp_sum(split_cols(front_upper_grad, 2))
    front_lower_grad = dp_sum(front_lower_grad)
    first_grad = second_grad + summed_y(back)
    mb = first_grad.astype(BF)
    mixes_grad = down_back(mb, mo)
    mixer_output_grad = dp_sum(contract_rows(four_wide(mixes), four_own(mb)))
    conv_pieces, kernel_grad = conv_backward(mixes_grad, projected, convolved, padded, mixer_kernel)
    width = mixer_kernel.shape[1]
    normed_one_grad = up_back([conv_pieces[:, i * width : (i + 1) * width] for i in range(3)], mi)
    mixer_gain_grad = jnp.sum(normed_one_grad * normed_one, axis=0)
    back = norm_backward(normed_one_grad, normed_one, scaling_one, gains[0])
    stream_grad = cotangent + bring_back(back + 0.25 * (first_grad - cot))
    input_grad = dp_sum(split_cols(contract_rows(four_own(inputs_one), four_wide(conv_pieces)), 3))

    gain_rows = jnp.stack([mixer_gain_grad, front_gain_grad, attend_gain_grad, rear_gain_grad])
    head_row = jnp.pad(jnp.concatenate([qgain_grad, kgain_grad]), (0, width - 2 * HD))[None]
    own, near, far, last = blocks(gain_rows)
    got = from_core(jnp.concatenate([near, last, kernel_grad, head_row], axis=0))
    sums = jnp.concatenate([own, far, kernel_grad, head_row], axis=0) + got
    got = from_facing(sums[4:])
    sums = jnp.concatenate([sums[:4], sums[8:]], axis=0) + got
    sums = sums + from_xl(sums)
    sums = sums + from_z(sums, 1) + from_z(sums, 2) + from_z(sums, 3)
    over_y = jnp.concatenate([sums[:4], sums[7:]], axis=0)
    over_y = over_y + from_y(over_y, 1) + from_y(over_y, 2) + from_y(over_y, 3)
    return (
        fourth,
        stream_grad,
        over_y[0],
        input_grad.reshape(mixer_input.shape),
        sums[4:7],
        mixer_output_grad,
        over_y[1],
        front_upper_grad.reshape(front_upper.shape),
        front_lower_grad,
        over_y[2],
        attend_query_grad,
        keyval_grad,
        over_y[4, :HD],
        over_y[4, HD : 2 * HD],
        attend_output_grad,
        over_y[3],
        rear_upper_grad.reshape(rear_upper.shape),
        rear_lower_grad,
    )


def solution(mesh):
    parts = Mesh(mesh.devices.reshape(4, 2, 2, 2, 4), ("z", "xl", "xh", "core", "y"))
    tokens = ("z", "xl", "y")
    row = ("xh", "core")
    stream = P(tokens, row)
    gain = P(row)
    upper = P(None, row, "y")
    lower = P("y", row)
    weights = (
        gain,
        upper,
        P(None, "y"),
        lower,
        gain,
        upper,
        lower,
        gain,
        P(row, "y"),
        upper,
        P(),
        P(),
        lower,
        gain,
        upper,
        lower,
    )
    return jax.shard_map(
        body,
        mesh=parts,
        in_specs=(stream, stream) + weights,
        out_specs=(stream, stream) + weights,
        check_vma=False,
    )
```

```python
import functools

import jax
import jax.numpy as jnp
from jax import lax
from jax.experimental import pallas as pl
from jax.experimental.pallas import tpu as pltpu
from jax.sharding import Mesh
from jax.sharding import PartitionSpec as P

D = 1024
HD = 64
KW = 3


EPS = 1e-05
THETA = 1000000.0
MASKED = -1e30

def contract_cols(left, right):
    return lax.dot_general(
        left, right, (((1,), (1,)), ((), ())), preferred_element_type=jnp.float32
    )


def rope_tables(length):
    half = HD // 2
    freqs = jnp.power(THETA, -(jnp.arange(half, dtype=jnp.float32) * 2.0 / HD))
    angles = jnp.arange(length, dtype=jnp.float32)[:, None] * freqs[None, :]
    cosine = jnp.concatenate([jnp.cos(angles), jnp.cos(angles)], axis=1)[:, None, :]
    sine = jnp.concatenate([jnp.sin(angles), jnp.sin(angles)], axis=1)[:, None, :]
    return (cosine, sine)


BF = jnp.bfloat16
F32 = jnp.float32


def xor_pairs(count, bits):
    return [(i, i ^ bits) for i in range(count)]


def from_core(x):
    return lax.ppermute(x, "core", xor_pairs(2, 1))


def from_facing(x):
    return lax.ppermute(x, ("xl", "xh"), xor_pairs(4, 3))


def from_xl(x):
    return lax.ppermute(x, "xl", xor_pairs(2, 1))


def from_z(x, bits):
    return lax.ppermute(x, "z", xor_pairs(4, bits))


def from_y(x, bits):
    return lax.ppermute(x, "y", xor_pairs(4, bits))


def gathered(shard):
    facing = from_facing(shard)
    others = from_core(jnp.stack([shard, facing]))
    return [shard, others[0], facing, others[1]]


def facing_half(halves):
    return from_facing(lax.dynamic_index_in_dim(halves, lax.axis_index("xl"), 0, keepdims=False))


def with_facing(halves, got, other):
    first = lax.axis_index("xl") == 0
    facing = jnp.stack([jnp.where(first, other, got), jnp.where(first, got, other)])
    return [halves, from_core(halves), facing, from_core(facing)]


def gathered_apart(shard):
    return lax.all_gather(shard, ("xh", "core"), axis=0, tiled=False)


def over_y(sent):
    return [sent] + [from_y(sent, bits) for bits in (1, 3, 2)]


def summed_y(x):
    return sum(part.astype(F32) for part in over_y(x.astype(BF)))


def blocks(x):
    width = x.shape[1] // 4
    return [x[:, i * width : (i + 1) * width] for i in range(4)]


def xor_order(parts, index):
    low = (index & 1) == 1
    high = (index & 2) == 2
    a = [jnp.where(low, parts[i ^ 1], parts[i]) for i in range(4)]
    return [jnp.where(high, a[i ^ 2], a[i]) for i in range(4)]


def place():
    return lax.axis_index("xh") * 2 + lax.axis_index("core"), lax.axis_index("y")


def own_order(x):
    return xor_order(blocks(x), place()[0])


def whole_order(parts):
    return jnp.concatenate(xor_order(parts, place()[0]), axis=1)


def spread_in(arrays):
    col = place()[1]
    x = jnp.concatenate(arrays, axis=1).astype(BF)
    parts = []
    for bits in range(4):
        pairs = [(w * 4 + s, s * 4 + (w ^ bits)) for w in range(4) for s in range(4)]
        parts.append(lax.ppermute(x, ("xh", "core", "y"), pairs))
    parts = xor_order(parts, col)
    return [
        jnp.concatenate([part[:, i * 256 : (i + 1) * 256] for part in parts], axis=1).astype(F32)
        for i in range(len(arrays))
    ]


def bring_back(arrays):
    parts = [jnp.concatenate(at, axis=1) for at in zip(*[blocks(x) for x in arrays])]
    total = None
    for bits in range(4):
        pairs = [(s * 4 + c, (c ^ bits) * 4 + s) for s in range(4) for c in range(4)]
        got = lax.ppermute(parts[bits], ("xh", "core", "y"), pairs).astype(F32)
        total = got if total is None else total + got
    return [total[:, i * 256 : (i + 1) * 256] for i in range(len(arrays))]


def widen(x, count):
    rows = x.shape[0] // count
    return jnp.concatenate([x[i * rows : (i + 1) * rows] for i in range(count)], axis=1)


def dp_sum_begun(g):
    z = lax.axis_index("z")
    g = g.astype(BF)
    quarter = g.shape[0] // 4

    def chunk(at):
        return lax.dynamic_slice_in_dim(g, at * quarter, quarter, 0)

    total = chunk(z).astype(F32)
    for bits in (1, 3, 2):
        total = total + from_z(chunk(z ^ bits), bits).astype(F32)
    return total.astype(BF)


def dp_sum_ended(sent):
    return gathered_z_directly(plus_xl(sent))


def dot(left, right):
    return jnp.dot(left, right, preferred_element_type=F32)


TILE = 384
VMEM = 56 * 2**20


def kernel_order(parts, bits):
    low = (bits & 1) == 1
    high = (bits & 2) == 2
    a = [jnp.where(low, parts[i ^ 1], parts[i]) for i in range(4)]
    return [jnp.where(high, a[i ^ 2], a[i]) for i in range(4)]


def plus_parts(base_ref, part_refs):
    total = base_ref[...]
    for ref in part_refs:
        total = total + ref[...].astype(F32)
    return total


def scaling_of(values):
    return lax.rsqrt(jnp.mean(values * values, axis=1, keepdims=True) + EPS)


def ffn_kernel(forward, backward, upper_apart, *refs):
    refs = list(refs)

    def take(count):
        out = refs[:count]
        del refs[:count]
        return out

    bits = refs.pop(0)[0]
    gain_ref = refs.pop(0)
    stream_ref = refs.pop(0)
    stream_parts = take(4) if forward else []
    if backward:
        back_ref = refs.pop(0)
        back_parts = [] if forward else take(4)
    if backward and not forward:
        gating_in, upward_in, hidden_in = take(3)
    uppers = take(4)
    lowers = take(4)
    if forward:
        stream_out, partial_out = take(2)
    if backward and not forward:
        total_out = refs.pop(0)
    if forward and not backward:
        gating_out, upward_out, hidden_out = take(3)
    if backward:
        facing_out, near_out, own_out, back_out, gain_out = take(5)
    n_ref = refs.pop(0)
    if forward:
        down_ref = refs.pop(0)
    if backward:
        c_ref, grad_ref = take(2)
    step = pl.program_id(0)
    last = pl.num_programs(0) - 1

    def cut(x):
        return [x[:, i * 256 : (i + 1) * 256] for i in range(4)]

    def upper(i, member):
        return uppers[i][0, member] if upper_apart else uppers[i][member]

    def apart(parts):
        return parts if upper_apart else kernel_order(parts, bits)

    @pl.when(step == 0)
    def _():
        if forward:
            stream = plus_parts(stream_ref, stream_parts)
            stream_out[...] = stream
        else:
            stream = stream_ref[...]
        normed = (stream * scaling_of(stream) * gain_ref[...]).astype(BF)
        if forward:
            for i, part in enumerate(apart(cut(normed))):
                n_ref[:, i * 256 : (i + 1) * 256] = part
            down_ref[...] = jnp.zeros_like(down_ref)
        if backward:
            upstream = plus_parts(back_ref, back_parts)
            if not forward:
                total_out[...] = upstream
            cs = kernel_order(cut(upstream.astype(BF)), bits)
            ns = kernel_order(cut(normed), bits)
            for i in range(4):
                c_ref[:, i * 256 : (i + 1) * 256] = cs[i]
            grad_ref[...] = jnp.zeros_like(grad_ref)
            own_out[:, :256] = ns[0]
            own_out[:, 256:] = cs[0]
            near_out[:, :256] = ns[1]
            near_out[:, 256:512] = cs[1]
            for i in (2, 3):
                facing_out[:, (i - 2) * 512 : (i - 2) * 512 + 256] = ns[i]
                facing_out[:, (i - 2) * 512 + 256 : (i - 1) * 512] = cs[i]

    if forward:
        gating = jnp.zeros((n_ref.shape[0], TILE), F32)
        upward = gating
        for i, part in enumerate(cut(n_ref)):
            gating += dot(part, upper(i, 0))
            upward += dot(part, upper(i, 1))
        hidden = (gating * jax.nn.sigmoid(gating) * upward).astype(BF)
        for i in range(4):
            down_ref[:, i * 256 : (i + 1) * 256] += dot(hidden, lowers[i][...])
        if not backward:
            gating_out[...] = gating
            upward_out[...] = upward
            hidden_out[...] = hidden

        @pl.when(step == last)
        def _():
            for i, part in enumerate(kernel_order(cut(down_ref), bits)):
                partial_out[:, i * 256 : (i + 1) * 256] = part.astype(BF)

    if backward:
        if not forward:
            gating, upward, hidden = gating_in[...], upward_in[...], hidden_in[...]
        hidden_grad = jnp.zeros((c_ref.shape[0], TILE), F32)
        for i, part in enumerate(cut(c_ref)):
            hidden_grad += contract_cols(part, lowers[i][...])
        sigmoid = jax.nn.sigmoid(gating)
        gating_grad = (hidden_grad * upward * sigmoid * (1.0 + gating * (1.0 - sigmoid))).astype(BF)
        upward_grad = (hidden_grad * gating * sigmoid).astype(BF)
        for i in range(4):
            grad_ref[:, i * 256 : (i + 1) * 256] += contract_cols(
                gating_grad, upper(i, 0)
            ) + contract_cols(upward_grad, upper(i, 1))
        for at, piece in enumerate((gating_grad, upward_grad, hidden)):
            place_at = at * 1152 + step * TILE
            near_out[:, pl.ds(pl.multiple_of(512 + place_at, 128), TILE)] = piece
            facing_out[:, pl.ds(pl.multiple_of(1024 + place_at, 128), TILE)] = piece

        @pl.when(step == last)
        def _():
            stream = stream_out[...] if forward else stream_ref[...]
            scaling = scaling_of(stream)
            normed = stream * scaling
            grad = jnp.concatenate(apart(cut(grad_ref)), axis=1)
            gain_out[...] = jnp.sum(grad * normed, axis=0, keepdims=True)
            grad = grad * gain_ref[...]
            inner = jnp.mean(grad * normed, axis=1, keepdims=True)
            back_out[...] = (scaling * (grad - normed * inner)).astype(BF)


def whole(shape):
    return pl.BlockSpec(shape, lambda *_: (0,) * len(shape))


def ffn(forward, backward, bits, gain, stream, stream_parts, back, back_parts, saved, upper, lower):
    rows, width = stream.shape
    hidden = lower[0].shape[0]
    upper_apart = not isinstance(upper, list)


    def tiles():
        return pl.BlockSpec((rows, TILE), lambda t: (0, t))

    stream_spec = whole((rows, width))
    args = [bits, gain, stream]
    specs = [pl.BlockSpec(memory_space=pltpu.SMEM), whole((1, width)), stream_spec]
    if forward:
        args += stream_parts
        specs += [stream_spec] * 4
    if backward:
        args += [back]
        specs += [stream_spec]
        if not forward:
            args += back_parts + saved
            specs += [stream_spec] * 4 + [tiles()] * 3
    if upper_apart:
        args += [upper] * 4
        specs += [
            pl.BlockSpec((1, 2, 256, TILE), lambda t, i=i: (i, 0, 0, t)) for i in range(4)
        ]
    else:
        args += upper
        specs += [pl.BlockSpec((2, 256, TILE), lambda t: (0, 0, t))] * 4
    args += lower
    specs += [pl.BlockSpec((TILE, 256), lambda t: (t, 0))] * 4
    outs, out_specs = [], []

    def out(shape, dtype, spec=None):
        outs.append(jax.ShapeDtypeStruct(shape, dtype))
        out_specs.append(whole(shape) if spec is None else spec)

    scratch = [pltpu.VMEM((rows, width), BF)]
    if forward:
        out((rows, width), F32)
        out((rows, width), BF)
        scratch += [pltpu.VMEM((rows, width), F32)]
    if backward and not forward:
        out((rows, width), F32)
    if forward and not backward:
        out((rows, hidden), F32, tiles())
        out((rows, hidden), F32, tiles())
        out((rows, hidden), BF, tiles())
    if backward:
        out((rows, 1024 + 3 * hidden), BF)
        out((rows, 512 + 3 * hidden), BF)
        out((rows, 512), BF)
        out((rows, width), BF)
        out((1, width), F32)
        scratch += [pltpu.VMEM((rows, width), BF), pltpu.VMEM((rows, width), F32)]
    flops = rows * width * hidden * 6 * (int(forward) + int(backward))
    return pl.pallas_call(
        functools.partial(ffn_kernel, forward, backward, upper_apart),
        grid=(hidden // TILE,),
        in_specs=specs,
        out_shape=outs,
        out_specs=out_specs,
        scratch_shapes=scratch,
        compiler_params=pltpu.CompilerParams(vmem_limit_bytes=VMEM),
        cost_estimate=pl.CostEstimate(
            flops=flops, bytes_accessed=12 * 2**20, transcendentals=rows * hidden
        ),
    )(*args)


def grads_kernel(tile, upper_steps, own_ref, mine_ref, near_ref, facing_ref, far_ref, out_ref, nt_ref, c_ref):
    step = pl.program_id(0)
    seqs = [(own_ref, 0), (near_ref, 0), (facing_ref, 0), (far_ref, 512)]

    @pl.when(step == 0)
    def _():
        for i, (ref, at) in enumerate(seqs):
            nt_ref[:, i * 128 : (i + 1) * 128] = ref[:, at : at + 256].T
            c_ref[i * 128 : (i + 1) * 128, :] = ref[:, at + 256 : at + 512]

    def columns(ref, start):
        return ref[:, pl.ds(pl.multiple_of(start + step * tile, 128), tile)]

    rows = jnp.concatenate(
        [
            columns(mine_ref, 512),
            columns(near_ref, 512),
            columns(facing_ref, 1024),
            columns(far_ref, 1024),
        ],
        axis=0,
    )

    @pl.when(step < upper_steps)
    def _():
        grad = dot(nt_ref[...], rows).astype(BF)
        for i in range(tile // 128):
            out_ref[i * 256 : (i + 1) * 256, :] = grad[:, i * 128 : (i + 1) * 128]

    @pl.when(step >= upper_steps)
    def _():
        grad = dot(rows.T, c_ref[...]).astype(BF)
        for i in range(2):
            out_ref[i * tile : (i + 1) * tile, :] = grad[:, i * 128 : (i + 1) * 128]


def weight_grads(tile, upper_steps, own, mine, near, facing, far):
    steps = (mine.shape[1] - 512) // tile
    return pl.pallas_call(
        functools.partial(grads_kernel, tile, upper_steps),
        grid=(steps,),
        in_specs=[whole(x.shape) for x in (own, mine, near, facing, far)],
        out_shape=jax.ShapeDtypeStruct((steps * 2 * tile, 128), BF),
        out_specs=pl.BlockSpec((2 * tile, 128), lambda t: (t, 0)),
        scratch_shapes=[pltpu.VMEM((256, 512), BF), pltpu.VMEM((512, 256), BF)],
        compiler_params=pltpu.CompilerParams(vmem_limit_bytes=VMEM),
        cost_estimate=pl.CostEstimate(
            flops=2 * 512 * 256 * steps * tile, bytes_accessed=7 * 2**20, transcendentals=0
        ),
    )(own, mine, near, facing, far)


def unpacked(grads, tile, steps, first):
    part = grads[first * 2 * tile : (first + steps) * 2 * tile]
    return widen(part, steps * tile // 128).astype(F32)


def unpacked_lower(grads, tile, first):
    part = grads[first * 2 * tile : (first + 1) * 2 * tile]
    return widen(part, 2).astype(F32)


def cut_blocks(x):
    return [x[:, i * 256 : (i + 1) * 256] for i in range(4)]


def store_blocks(ref, parts, start=0):
    at = start
    for part in parts:
        ref[:, at : at + part.shape[1]] = part.astype(ref.dtype)
        at += part.shape[1]


def lanes_of(x):
    return lax.broadcasted_iota(jnp.int32, x.shape, 1)


def rows_of(x):
    return lax.broadcasted_iota(jnp.int32, x.shape, 0)


def rotated(u):
    width = u.shape[1]
    first = lanes_of(u) % HD < HD // 2
    return jnp.where(first, -pltpu.roll(u, width - HD // 2, 1), pltpu.roll(u, HD // 2, 1))


def head_means(u):
    lanes = lanes_of(u) // HD
    out = jnp.zeros_like(u)
    for head in range(u.shape[1] // HD):
        mine = lanes == head
        total = jnp.sum(jnp.where(mine, u, 0.0), axis=1, keepdims=True)
        out = jnp.where(mine, total / HD, out)
    return out


def heads_turned(u, gain, cosine, sine):
    scaling = lax.rsqrt(head_means(u * u) + EPS)
    normed = u * scaling
    scaled = normed * gain
    return normed, scaling, scaled * cosine + rotated(scaled) * sine


def heads_back(grad, normed, scaling, gain, cosine, sine):
    du = grad * cosine - rotated(grad * sine)
    gain_grad = jnp.sum(du * normed, axis=0, keepdims=True)
    scaled = du * gain
    return scaling * (scaled - normed * head_means(scaled * normed)), gain_grad


def both_places(x):
    return x.astype(BF), pltpu.roll(x, HD, 1).astype(BF)


def one_head(x, at):
    return jnp.where(lanes_of(x) // HD == at, x, jnp.zeros_like(x))


def side_by_side(left, right):
    return jnp.where(lanes_of(left) < HD, left, right)


def norm_grad(stream, grad, gain, gain_out):
    scaling = scaling_of(stream)
    normed = stream * scaling
    gain_out[...] = jnp.sum(grad * normed, axis=0, keepdims=True)
    grad = grad * gain
    inner = jnp.mean(grad * normed, axis=1, keepdims=True)
    return scaling * (grad - normed * inner)


def store_bundles(ns, cs, wides, facing_out, near_out, own_out):
    store_blocks(own_out, [ns[0], cs[0]])
    store_blocks(near_out, [ns[1], cs[1]] + wides)
    store_blocks(facing_out, [ns[2], cs[2], ns[3], cs[3]] + wides)


def attend_forward_kernel(
    bits_ref, gain_ref, qgain_ref, kgain_ref, cos_ref, sin_ref, base_ref, p0, p1, p2, p3, w0, w1, w2, w3,
    stream_out, partial_out, projected_out, probs_out, att_out,
):
    bits = bits_ref[0]
    weights = (w0, w1, w2, w3)
    stream = plus_parts(base_ref, (p0, p1, p2, p3))
    stream_out[...] = stream
    normed = (stream * scaling_of(stream) * gain_ref[...]).astype(BF)
    projected = jnp.zeros((128, 512), F32)
    for part, weight in zip(kernel_order(cut_blocks(normed), bits), weights):
        projected += dot(part, weight[:, :512])
    projected_out[...] = projected
    cosine, sine = cos_ref[...], sin_ref[...]
    query = heads_turned(projected[:, :256], qgain_ref[...], cosine, sine)[2].astype(BF)
    keys = heads_turned(projected[:, 256:384], kgain_ref[...], cosine[:, :128], sine[:, :128])[2]
    keys = both_places(keys)
    values = both_places(projected[:, 384:])
    causal = rows_of(probs_out[:, :128]) >= lanes_of(probs_out[:, :128])
    for kv in range(2):
        block = query[:, kv * 128 : (kv + 1) * 128]
        mixed = []
        for at in range(2):
            scores = contract_cols(one_head(block, at), keys[at ^ kv]) * HD ** (-0.5)
            scores = jnp.where(causal, scores, MASKED)
            peak = jnp.max(scores, axis=1, keepdims=True)
            logsum = peak + jnp.log(jnp.sum(jnp.exp(scores - peak), axis=1, keepdims=True))
            probs = jnp.exp(scores - logsum)
            head = kv * 2 + at
            probs_out[:, head * 128 : (head + 1) * 128] = probs
            mixed.append(dot(probs.astype(BF), values[at ^ kv]))
        att_out[:, kv * 128 : (kv + 1) * 128] = side_by_side(*mixed).astype(BF)
    att = att_out[...]
    outs = [dot(att, weight[:, 512:]) for weight in weights]
    store_blocks(partial_out, kernel_order(outs, bits))


def attend_backward_kernel(
    bits_ref, gain_ref, qgain_ref, kgain_ref, cos_ref, sin_ref, stream_ref, base_ref, p0, p1, p2, p3,
    projected_ref, probs_ref, att_ref, w0, w1, w2, w3,
    total_out, facing_out, near_out, own_out, back_out, gain_out, qgain_out, kgain_out,
):
    bits = bits_ref[0]
    weights = (w0, w1, w2, w3)
    total = plus_parts(base_ref, (p0, p1, p2, p3))
    total_out[...] = total
    cs = kernel_order(cut_blocks(total.astype(BF)), bits)
    grad = jnp.zeros((128, 256), F32)
    for part, weight in zip(cs, weights):
        grad += contract_cols(part, weight[:, 512:])
    grad = grad.astype(BF)
    cosine, sine = cos_ref[...], sin_ref[...]
    projected = projected_ref[...]
    qnormed, qscaling, query = heads_turned(projected[:, :256], qgain_ref[...], cosine, sine)
    query = query.astype(BF)
    knormed, kscaling, keys = heads_turned(
        projected[:, 256:384], kgain_ref[...], cosine[:, :128], sine[:, :128]
    )
    keys = both_places(keys)
    values = both_places(projected[:, 384:])
    dquery, dkeys, dvalues = [], [], []
    for kv in range(2):
        block = query[:, kv * 128 : (kv + 1) * 128]
        gblock = grad[:, kv * 128 : (kv + 1) * 128]
        dqs = []
        dk = jnp.zeros((128, 128), F32)
        dv = jnp.zeros((128, 128), F32)
        for at in range(2):
            head = kv * 2 + at
            probs = probs_ref[:, head * 128 : (head + 1) * 128]
            mine = one_head(gblock, at)
            dv += dot(probs.T.astype(BF), mine)
            dprobs = contract_cols(mine, values[at ^ kv])
            delta = jnp.sum(probs * dprobs, axis=1, keepdims=True)
            dscores = probs * (dprobs - delta)
            dqs.append(dot(dscores.astype(BF), keys[at ^ kv]))
            dk += dot(dscores.T.astype(BF), one_head(block, at))
        dquery.append(side_by_side(*dqs) * HD ** (-0.5))
        dkeys.append((dk + pltpu.roll(dk, HD, 1)) * HD ** (-0.5))
        dvalues.append(dv + pltpu.roll(dv, HD, 1))
    dquery = jnp.concatenate(dquery, axis=1)
    dquery, qgain = heads_back(dquery, qnormed, qscaling, qgain_ref[...], cosine, sine)
    dkeys, kgain = heads_back(
        side_by_side(*dkeys), knormed, kscaling, kgain_ref[...], cosine[:, :128], sine[:, :128]
    )
    qgain_out[...] = qgain
    kgain_out[...] = kgain
    pieces = jnp.concatenate([dquery, dkeys, side_by_side(*dvalues)], axis=1).astype(BF)
    outs = [contract_cols(pieces, weight[:, :512]) for weight in weights]
    grad = jnp.concatenate(kernel_order(outs, bits), axis=1)
    stream = stream_ref[...]
    back_out[...] = norm_grad(stream, grad, gain_ref[...], gain_out).astype(BF)
    normed = (stream * scaling_of(stream) * gain_ref[...]).astype(BF)
    ns = kernel_order(cut_blocks(normed), bits)
    store_bundles(ns, cs, [pieces, att_ref[...]], facing_out, near_out, own_out)


def shifted_down(x, count):
    if count == 0:
        return x
    return jnp.where(rows_of(x) >= count, pltpu.roll(x, count, 0), 0.0)


def shifted_up(x, count):
    if count == 0:
        return x
    rows = x.shape[0]
    return jnp.where(rows_of(x) < rows - count, pltpu.roll(x, rows - count, 0), 0.0)


def mixer_weights(own_in, core_in, low, high, core_low, core_high, own_out, core_out):
    ins = [
        [own_in[k], core_in[k], (low, high)[k // 2][k % 2], (core_low, core_high)[k // 2][k % 2]]
        for k in range(3)
    ]
    return ins, [own_out[...], core_out[...], high[1], core_high[1]]


def convolved(bx, taps_ref):
    return sum(shifted_down(bx, KW - 1 - k) * taps_ref[k : k + 1, :] for k in range(KW))


def mixer_forward_kernel(bits_ref, gain_ref, taps_ref, stream_ref, *refs):
    ins, outs = mixer_weights(*refs[:8])
    partial_out, projected_out, mix_out = refs[8:]
    bits = bits_ref[0]
    stream = stream_ref[...]
    normed = (stream * scaling_of(stream) * gain_ref[...]).astype(BF)
    ns = kernel_order(cut_blocks(normed), bits)
    projected = []
    for k in range(3):
        total = jnp.zeros((128, 256), F32)
        for part, weight in zip(ns, ins[k]):
            total += dot(part, weight)
        projected.append(total)
        projected_out[k] = total
    mix = (projected[1] * convolved(projected[0] * projected[2], taps_ref)).astype(BF)
    mix_out[...] = mix
    store_blocks(partial_out, kernel_order([dot(mix, weight) for weight in outs], bits))


def mixer_backward_kernel(
    bits_ref, gain_ref, taps_ref, stream_ref, base_ref, p0, p1, p2, p3, start_ref, projected_ref, mix_ref, *refs
):
    ins, outs = mixer_weights(*refs[:8])
    facing_out, near_out, own_out, back_out, gain_out, taps_out = refs[8:]
    bits = bits_ref[0]
    total = plus_parts(base_ref, (p0, p1, p2, p3))
    cs = kernel_order(cut_blocks(total.astype(BF)), bits)
    dmix = jnp.zeros((128, 256), F32)
    for part, weight in zip(cs, outs):
        dmix += contract_cols(part, weight)
    pb, pc, px = projected_ref[0], projected_ref[1], projected_ref[2]
    bx = pb * px
    dconv = dmix * pc
    for k in range(KW):
        taps_out[k : k + 1, :] = jnp.sum(
            dconv * shifted_down(bx, KW - 1 - k), axis=0, keepdims=True
        )
    dbx = sum(shifted_up(dconv, KW - 1 - k) * taps_ref[k : k + 1, :] for k in range(KW))
    pieces = [
        (dbx * px).astype(BF),
        (dmix * convolved(bx, taps_ref)).astype(BF),
        (dbx * pb).astype(BF),
    ]
    grads = []
    for i in range(4):
        grads.append(sum(contract_cols(pieces[k], ins[k][i]) for k in range(3)))
    grad = jnp.concatenate(kernel_order(grads, bits), axis=1)
    stream = stream_ref[...]
    back = norm_grad(stream, grad, gain_ref[...], gain_out) + 0.25 * (total - start_ref[...])
    store_blocks(back_out, kernel_order(cut_blocks(back.astype(BF)), bits_ref[1]))
    normed = (stream * scaling_of(stream) * gain_ref[...]).astype(BF)
    ns = kernel_order(cut_blocks(normed), bits)
    store_bundles(ns, cs, pieces + [mix_ref[...]], facing_out, near_out, own_out)


def in_one_step(kernel, args, outs, flops):
    return pl.pallas_call(
        kernel,
        grid=(1,),
        in_specs=[pl.BlockSpec(memory_space=pltpu.SMEM)] + [whole(x.shape) for x in args[1:]],
        out_shape=[jax.ShapeDtypeStruct(shape, dtype) for shape, dtype in outs],
        out_specs=[whole(shape) for shape, dtype in outs],
        compiler_params=pltpu.CompilerParams(vmem_limit_bytes=VMEM),
        cost_estimate=pl.CostEstimate(
            flops=flops, bytes_accessed=6 * 2**20, transcendentals=128 * 1024
        ),
    )(*args)


def tied(*values):
    return lax.optimization_barrier(values)


def unpack_kernel(in_ref, upper_out, lower_out):
    for k in range(2):
        for i in range(9):
            at = (k * 9 + i) * 256
            upper_out[k, :, i * 128 : (i + 1) * 128] = in_ref[at : at + 256, :].astype(F32)
    for i in range(3):
        for half in range(2):
            at = 18 * 256 + (i * 2 + half) * TILE
            lower_out[i * TILE : (i + 1) * TILE, half * 128 : (half + 1) * 128] = in_ref[
                at : at + TILE, :
            ].astype(F32)


def ffn_unpacked(grads):
    shapes = [(2, 256, 3 * TILE), (3 * TILE, 256)]
    return pl.pallas_call(
        unpack_kernel,
        grid=(1,),
        in_specs=[whole(grads.shape)],
        out_shape=[jax.ShapeDtypeStruct(shape, F32) for shape in shapes],
        out_specs=[whole(shape) for shape in shapes],
        compiler_params=pltpu.CompilerParams(vmem_limit_bytes=VMEM),
    )(grads)


def scattered_z(g):
    return lax.psum_scatter(g, "z", scatter_dimension=0, tiled=True)


def plus_xl(part):
    return (part.astype(F32) + from_xl(part).astype(F32)).astype(BF)


def gathered_z_directly(piece):
    pieces = [piece] + [from_z(piece, bits) for bits in (1, 2, 3)]
    return jnp.concatenate(xor_order(pieces, lax.axis_index("z")), axis=0)


def gathered_z(part):
    return lax.all_gather(part, "z", axis=0, tiled=True)


def body(
    stream_in,
    cotangent,
    mixer_gain,
    mixer_input,
    mixer_kernel,
    mixer_output,
    front_gain,
    front_upper,
    front_lower,
    attend_gain,
    attend_query,
    attend_keyval,
    query_gain,
    key_gain,
    attend_output,
    rear_gain,
    rear_upper,
    rear_lower,
):
    bits = place()[0].astype(jnp.int32).reshape(1)
    x, cot = spread_in([stream_in, cotangent])
    even = lax.axis_index("xl") == 0
    mixer_got = from_facing(
        jnp.where(
            even,
            mixer_input[:2],
            jnp.concatenate([mixer_input[2:], mixer_output[None]], axis=0),
        )
    )
    x, mixer_got, gains, front_upper, front_lower = tied(
        x,
        mixer_got,
        jnp.stack([mixer_gain, front_gain, attend_gain, rear_gain]),
        front_upper,
        front_lower,
    )
    gains = whole_order(gathered(gains))
    mixer_other = from_xl(mixer_got)
    fu = front_upper
    fu_got = facing_half(fu)
    fl_facing = from_facing(front_lower)
    low = jnp.where(even, mixer_other, mixer_got)
    high = jnp.where(even, mixer_got, mixer_other)
    core_input, core_output = from_core(mixer_input), from_core(mixer_output)
    core_low, core_high = from_core(low), from_core(high)
    mixer = [mixer_input, core_input, low, high, core_low, core_high, mixer_output, core_output]
    attend = jnp.concatenate(
        [attend_query, attend_keyval[0], attend_keyval[1], attend_output], axis=1
    )
    tokens, width = x.shape
    wide = (tokens, width)
    cosine, sine = rope_tables(tokens)
    tables = [
        gains[2:3],
        jnp.tile(query_gain, 4)[None],
        jnp.tile(key_gain, 2)[None],
        jnp.tile(cosine[:, 0], (1, 4)),
        jnp.tile(sine[:, 0], (1, 4)),
    ]
    partial, projected, mixes = in_one_step(
        mixer_forward_kernel,
        [bits, gains[:1], mixer_kernel, x] + mixer,
        [(wide, BF), ((3, tokens, 256), F32), ((tokens, 256), BF)],
        2 * tokens * width * 1024,
    )
    partial, fu_got = tied(partial, fu_got)
    parts = over_y(partial)
    fu_other = from_xl(fu_got)
    parts, fu_other, fl_facing, attend = tied(parts, fu_other, fl_facing, attend)
    attend_facing = from_facing(attend)
    attend_facing, rear_upper = tied(attend_facing, rear_upper)
    fu = with_facing(fu, fu_got, fu_other)
    fl = [front_lower, from_core(front_lower), fl_facing, from_core(fl_facing)]
    ru = gathered_apart(rear_upper)
    first, partial, *front_saved = ffn(
        True, False, bits, gains[1:2], x, parts, None, None, None, fu, fl
    )
    parts, attend_facing, rear_lower = tied(over_y(partial), attend_facing, rear_lower)
    attend = [attend, from_core(attend), attend_facing, from_core(attend_facing)]
    rl_facing = from_facing(rear_lower)
    second, partial, attn_projected, probs, attended = in_one_step(
        attend_forward_kernel,
        [bits] + tables + [first] + parts + attend,
        [
            (wide, F32),
            (wide, BF),
            ((tokens, 512), F32),
            ((tokens, 512), F32),
            ((tokens, 256), BF),
        ],
        2 * tokens * width * 1024,
    )
    parts, rl_facing = tied(over_y(partial), rl_facing)
    rl = [rear_lower, from_core(rear_lower), rl_facing, from_core(rl_facing)]
    third, partial, facing_bundle, near_bundle, own, back, rear_gain_grad = ffn(
        True, True, bits, gains[3:4], second, parts, cot, None, None, ru, rl
    )
    sent_out = jnp.concatenate(
        xor_order(blocks((partial.astype(F32) + 0.25 * (third - x)).astype(BF)), place()[1]), axis=1
    )
    rear_near = from_core(near_bundle)
    back_parts, facing_bundle = tied(over_y(back), facing_bundle)
    rear_facing = from_facing(facing_bundle)
    rear_mine, rear_own = near_bundle, own
    (
        third_grad,
        attn_facing,
        attn_mine,
        attn_own,
        sent,
        attend_gain_grad,
        qgain_grad,
        kgain_grad,
    ) = in_one_step(
        attend_backward_kernel,
        [bits] + tables + [second, cot] + back_parts + [attn_projected, probs, attended] + attend,
        [
            (wide, F32),
            ((tokens, 1792), BF),
            ((tokens, 1280), BF),
            ((tokens, 512), BF),
            (wide, BF),
            ((1, width), F32),
            ((1, 256), F32),
            ((1, 128), F32),
        ],
        4 * tokens * width * 1024,
    )
    qgain_grad = jnp.sum(qgain_grad.reshape(4, HD), axis=0)
    kgain_grad = jnp.sum(kgain_grad.reshape(2, HD), axis=0)
    parts, rear_facing = tied(over_y(sent), rear_facing)
    rear_grads = weight_grads(
        TILE, 6, rear_own, rear_mine, rear_near, rear_facing, from_core(rear_facing)
    )
    parts, rear_grads = tied(parts, rear_grads)
    rear_part = scattered_z(rear_grads)
    attn_near = from_core(attn_mine)
    attn_facing = from_facing(attn_facing)
    second_grad, facing_bundle, near_bundle, own, back, front_gain_grad = ffn(
        False, True, bits, gains[1:2], first, None, third_grad, parts, front_saved, fu, fl
    )
    parts = over_y(back)
    front_near = from_core(near_bundle)
    front_facing = from_facing(facing_bundle)
    parts, attn_facing, rear_part = tied(parts, attn_facing, rear_part)
    rear_part = plus_xl(rear_part)
    attn_far = from_core(attn_facing)
    mixer_facing, mixer_mine, mixer_own, stream_back, mixer_gain_grad, kernel_grad = in_one_step(
        mixer_backward_kernel,
        [jnp.stack(place()).astype(jnp.int32), gains[:1], mixer_kernel, x, second_grad]
        + parts
        + [cot, projected, mixes]
        + mixer,
        [
            ((tokens, 2048), BF),
            ((tokens, 1536), BF),
            ((tokens, 512), BF),
            (wide, BF),
            ((1, width), F32),
            ((KW, 256), F32),
        ],
        4 * tokens * width * 1024,
    )
    mixer_near = from_core(mixer_mine)
    mixer_facing = from_facing(mixer_facing)
    attn_grads = weight_grads(256, 2, attn_own, attn_mine, attn_near, attn_facing, attn_far)
    stream_back, front_facing, sent_out, rear_part, attn_grads = tied(
        stream_back, front_facing, sent_out, rear_part, attn_grads
    )
    front_grads = weight_grads(
        TILE, 6, own, near_bundle, front_near, front_facing, from_core(front_facing)
    )
    rear_all = gathered_z(rear_part)
    front_part = scattered_z(front_grads)
    sum_back, sum_out = bring_back([stream_back, sent_out])
    stream_grad = cotangent + sum_back
    fourth = stream_in + sum_out
    mixer_facing, stream_grad, fourth = tied(mixer_facing, stream_grad, fourth)
    mixer_grads = weight_grads(
        256, 3, mixer_own, mixer_mine, mixer_near, mixer_facing, from_core(mixer_facing)
    )
    sent = dp_sum_begun(jnp.concatenate([mixer_grads, attn_grads], axis=0))
    sent, front_part, rear_all = tied(sent, front_part, rear_all)
    front_part = plus_xl(front_part)
    small_grads = dp_sum_ended(sent)
    front_all = gathered_z(front_part)
    rear_upper_grad, rear_lower_grad = ffn_unpacked(rear_all)
    rear_upper_grad, rear_lower_grad, small_grads, front_all = tied(
        rear_upper_grad, rear_lower_grad, small_grads, front_all
    )
    cut = mixer_grads.shape[0]
    mixer_grads, attn_grads = small_grads[:cut], small_grads[cut:]
    input_grad = jnp.stack([unpacked(mixer_grads, 256, 1, k) for k in range(3)])
    mixer_output_grad = unpacked_lower(mixer_grads, 256, 3)
    attend_query_grad = unpacked(attn_grads, 256, 1, 0)
    keyval_grad = attn_grads[512:1024].astype(F32).reshape(2, 256, 128)
    attend_output_grad = unpacked_lower(attn_grads, 256, 2)
    front_upper_grad, front_lower_grad = ffn_unpacked(front_all)

    gain_rows = jnp.stack(
        [mixer_gain_grad[0], front_gain_grad[0], attend_gain_grad[0], rear_gain_grad[0]]
    )
    head_row = jnp.pad(jnp.concatenate([qgain_grad, kgain_grad]), (0, 256 - 2 * HD))[None]
    own, near, far, last = own_order(gain_rows)
    got = from_core(jnp.concatenate([near, last, kernel_grad, head_row], axis=0))
    sums = jnp.concatenate([own, far, kernel_grad, head_row], axis=0) + got
    got = from_facing(sums[4:])
    sums = jnp.concatenate([sums[:4], sums[8:]], axis=0) + got
    sums = sums + from_xl(sums)
    sums = sums + from_z(sums, 1) + from_z(sums, 2) + from_z(sums, 3)
    all_y = jnp.concatenate([sums[:4], sums[7:]], axis=0)
    all_y = all_y + from_y(all_y, 1) + from_y(all_y, 2) + from_y(all_y, 3)
    return (
        fourth,
        stream_grad,
        all_y[0],
        input_grad,
        sums[4:7],
        mixer_output_grad,
        all_y[1],
        front_upper_grad,
        front_lower_grad,
        all_y[2],
        attend_query_grad,
        keyval_grad,
        all_y[4, :HD],
        all_y[4, HD : 2 * HD],
        attend_output_grad,
        all_y[3],
        rear_upper_grad,
        rear_lower_grad,
    )


def solution(mesh):
    parts = Mesh(mesh.devices.reshape(4, 2, 2, 2, 4), ("z", "xl", "xh", "core", "y"))
    tokens = ("z", "xl", "y")
    row = ("xh", "core")
    stream = P(tokens, row)
    gain = P(row)
    upper = P(None, row, "y")
    lower = P("y", row)
    weights = (
        gain,
        upper,
        P(None, "y"),
        lower,
        gain,
        upper,
        lower,
        gain,
        P(row, "y"),
        upper,
        P(),
        P(),
        lower,
        gain,
        upper,
        lower,
    )
    return jax.shard_map(
        body,
        mesh=parts,
        in_specs=(stream, stream) + weights,
        out_specs=(stream, stream) + weights,
        check_vma=False,
    )
```

```python
import functools

import jax
import jax.numpy as jnp
from jax import lax
from jax.experimental import pallas as pl
from jax.experimental.pallas import tpu as pltpu
from jax.sharding import Mesh
from jax.sharding import PartitionSpec as P

D = 1024
HD = 64
KW = 3


EPS = 1e-05
THETA = 1000000.0
MASKED = -1e30

def contract_cols(left, right):
    return lax.dot_general(
        left, right, (((1,), (1,)), ((), ())), preferred_element_type=jnp.float32
    )


def rope_tables(length):
    half = HD // 2
    freqs = jnp.power(THETA, -(jnp.arange(half, dtype=jnp.float32) * 2.0 / HD))
    angles = jnp.arange(length, dtype=jnp.float32)[:, None] * freqs[None, :]
    cosine = jnp.concatenate([jnp.cos(angles), jnp.cos(angles)], axis=1)[:, None, :]
    sine = jnp.concatenate([jnp.sin(angles), jnp.sin(angles)], axis=1)[:, None, :]
    return (cosine, sine)


BF = jnp.bfloat16
F32 = jnp.float32


def xor_pairs(count, bits):
    return [(i, i ^ bits) for i in range(count)]


def from_core(x):
    return lax.ppermute(x, "core", xor_pairs(2, 1))


def from_facing(x):
    return lax.ppermute(x, ("xl", "xh"), xor_pairs(4, 3))


def from_xl(x):
    return lax.ppermute(x, "xl", xor_pairs(2, 1))


def from_z(x, bits):
    return lax.ppermute(x, "z", xor_pairs(4, bits))


def from_y(x, bits):
    return lax.ppermute(x, "y", xor_pairs(4, bits))


def gathered(shard):
    facing = from_facing(shard)
    others = from_core(jnp.stack([shard, facing]))
    return [shard, others[0], facing, others[1]]


def facing_half(halves):
    return from_facing(lax.dynamic_index_in_dim(halves, lax.axis_index("xl"), 0, keepdims=False))


def with_facing(halves, got, other):
    first = lax.axis_index("xl") == 0
    facing = jnp.stack([jnp.where(first, other, got), jnp.where(first, got, other)])
    return [halves, from_core(halves), facing, from_core(facing)]


def gathered_apart(shard):
    return lax.all_gather(shard, ("xh", "core"), axis=0, tiled=False)


def over_y(sent):
    return [sent] + [from_y(sent, bits) for bits in (1, 3, 2)]


def summed_y(x):
    return sum(part.astype(F32) for part in over_y(x.astype(BF)))


def blocks(x):
    width = x.shape[1] // 4
    return [x[:, i * width : (i + 1) * width] for i in range(4)]


def xor_order(parts, index):
    low = (index & 1) == 1
    high = (index & 2) == 2
    a = [jnp.where(low, parts[i ^ 1], parts[i]) for i in range(4)]
    return [jnp.where(high, a[i ^ 2], a[i]) for i in range(4)]


def place():
    return lax.axis_index("xh") * 2 + lax.axis_index("core"), lax.axis_index("y")


def own_order(x):
    return xor_order(blocks(x), place()[0])


def whole_order(parts):
    return jnp.concatenate(xor_order(parts, place()[0]), axis=1)


def spread_in(arrays):
    col = place()[1]
    x = jnp.concatenate(arrays, axis=1).astype(BF)
    parts = []
    for bits in range(4):
        pairs = [(w * 4 + s, s * 4 + (w ^ bits)) for w in range(4) for s in range(4)]
        parts.append(lax.ppermute(x, ("xh", "core", "y"), pairs))
    parts = xor_order(parts, col)
    return [
        jnp.concatenate([part[:, i * 256 : (i + 1) * 256] for part in parts], axis=1).astype(F32)
        for i in range(len(arrays))
    ]


def bring_back(arrays):
    parts = [jnp.concatenate(at, axis=1) for at in zip(*[blocks(x) for x in arrays])]
    total = None
    for bits in range(4):
        pairs = [(s * 4 + c, (c ^ bits) * 4 + s) for s in range(4) for c in range(4)]
        got = lax.ppermute(parts[bits], ("xh", "core", "y"), pairs).astype(F32)
        total = got if total is None else total + got
    return [total[:, i * 256 : (i + 1) * 256] for i in range(len(arrays))]


def widen(x, count):
    rows = x.shape[0] // count
    return jnp.concatenate([x[i * rows : (i + 1) * rows] for i in range(count)], axis=1)


def dp_sum_begun(g):
    z = lax.axis_index("z")
    g = g.astype(BF)
    quarter = g.shape[0] // 4

    def chunk(at):
        return lax.dynamic_slice_in_dim(g, at * quarter, quarter, 0)

    total = chunk(z).astype(F32)
    for bits in (1, 3, 2):
        total = total + from_z(chunk(z ^ bits), bits).astype(F32)
    return total.astype(BF)


def dp_sum_ended(sent):
    return gathered_z_directly(plus_xl(sent))


def dot(left, right):
    return jnp.dot(left, right, preferred_element_type=F32)


TILE = 384
VMEM = 56 * 2**20


def kernel_order(parts, bits):
    low = (bits & 1) == 1
    high = (bits & 2) == 2
    a = [jnp.where(low, parts[i ^ 1], parts[i]) for i in range(4)]
    return [jnp.where(high, a[i ^ 2], a[i]) for i in range(4)]


def plus_parts(base_ref, part_refs):
    total = base_ref[...]
    for ref in part_refs:
        total = total + ref[...].astype(F32)
    return total


def scaling_of(values):
    return lax.rsqrt(jnp.mean(values * values, axis=1, keepdims=True) + EPS)


def ffn_kernel(forward, backward, upper_apart, *refs):
    refs = list(refs)

    def take(count):
        out = refs[:count]
        del refs[:count]
        return out

    bits = refs.pop(0)[0]
    gain_ref = refs.pop(0)
    stream_ref = refs.pop(0)
    stream_parts = take(4) if forward else []
    if backward:
        back_ref = refs.pop(0)
        back_parts = [] if forward else take(4)
    if backward and not forward:
        gating_in, upward_in, hidden_in = take(3)
    uppers = take(4)
    lowers = take(4)
    if forward:
        stream_out, partial_out = take(2)
    if backward and not forward:
        total_out = refs.pop(0)
    if forward and not backward:
        gating_out, upward_out, hidden_out = take(3)
    if backward:
        facing_out, near_out, own_out, back_out, gain_out = take(5)
    n_ref = refs.pop(0)
    if forward:
        down_ref = refs.pop(0)
    if backward:
        c_ref, grad_ref = take(2)
    step = pl.program_id(0)
    last = pl.num_programs(0) - 1

    def cut(x):
        return [x[:, i * 256 : (i + 1) * 256] for i in range(4)]

    def upper(i, member):
        return uppers[i][0, member] if upper_apart else uppers[i][member]

    def apart(parts):
        return parts if upper_apart else kernel_order(parts, bits)

    @pl.when(step == 0)
    def _():
        if forward:
            stream = plus_parts(stream_ref, stream_parts)
            stream_out[...] = stream
        else:
            stream = stream_ref[...]
        normed = (stream * scaling_of(stream) * gain_ref[...]).astype(BF)
        if forward:
            for i, part in enumerate(apart(cut(normed))):
                n_ref[:, i * 256 : (i + 1) * 256] = part
            down_ref[...] = jnp.zeros_like(down_ref)
        if backward:
            upstream = plus_parts(back_ref, back_parts)
            if not forward:
                total_out[...] = upstream
            cs = kernel_order(cut(upstream.astype(BF)), bits)
            ns = kernel_order(cut(normed), bits)
            for i in range(4):
                c_ref[:, i * 256 : (i + 1) * 256] = cs[i]
            grad_ref[...] = jnp.zeros_like(grad_ref)
            own_out[:, :256] = ns[0]
            own_out[:, 256:] = cs[0]
            near_out[:, :256] = ns[1]
            near_out[:, 256:512] = cs[1]
            for i in (2, 3):
                facing_out[:, (i - 2) * 512 : (i - 2) * 512 + 256] = ns[i]
                facing_out[:, (i - 2) * 512 + 256 : (i - 1) * 512] = cs[i]

    if forward:
        gating = jnp.zeros((n_ref.shape[0], TILE), F32)
        upward = gating
        for i, part in enumerate(cut(n_ref)):
            gating += dot(part, upper(i, 0))
            upward += dot(part, upper(i, 1))
        hidden = (gating * jax.nn.sigmoid(gating) * upward).astype(BF)
        for i in range(4):
            down_ref[:, i * 256 : (i + 1) * 256] += dot(hidden, lowers[i][...])
        if not backward:
            gating_out[...] = gating
            upward_out[...] = upward
            hidden_out[...] = hidden

        @pl.when(step == last)
        def _():
            for i, part in enumerate(kernel_order(cut(down_ref), bits)):
                partial_out[:, i * 256 : (i + 1) * 256] = part.astype(BF)

    if backward:
        if not forward:
            gating, upward, hidden = gating_in[...], upward_in[...], hidden_in[...]
        hidden_grad = jnp.zeros((c_ref.shape[0], TILE), F32)
        for i, part in enumerate(cut(c_ref)):
            hidden_grad += contract_cols(part, lowers[i][...])
        sigmoid = jax.nn.sigmoid(gating)
        gating_grad = (hidden_grad * upward * sigmoid * (1.0 + gating * (1.0 - sigmoid))).astype(BF)
        upward_grad = (hidden_grad * gating * sigmoid).astype(BF)
        for i in range(4):
            grad_ref[:, i * 256 : (i + 1) * 256] += contract_cols(
                gating_grad, upper(i, 0)
            ) + contract_cols(upward_grad, upper(i, 1))
        for at, piece in enumerate((gating_grad, upward_grad, hidden)):
            place_at = at * 1152 + step * TILE
            near_out[:, pl.ds(pl.multiple_of(512 + place_at, 128), TILE)] = piece
            facing_out[:, pl.ds(pl.multiple_of(1024 + place_at, 128), TILE)] = piece

        @pl.when(step == last)
        def _():
            stream = stream_out[...] if forward else stream_ref[...]
            scaling = scaling_of(stream)
            normed = stream * scaling
            grad = jnp.concatenate(apart(cut(grad_ref)), axis=1)
            gain_out[...] = jnp.sum(grad * normed, axis=0, keepdims=True)
            grad = grad * gain_ref[...]
            inner = jnp.mean(grad * normed, axis=1, keepdims=True)
            back_out[...] = (scaling * (grad - normed * inner)).astype(BF)


def whole(shape):
    return pl.BlockSpec(shape, lambda *_: (0,) * len(shape))


def ffn(forward, backward, bits, gain, stream, stream_parts, back, back_parts, saved, upper, lower):
    rows, width = stream.shape
    hidden = lower[0].shape[0]
    upper_apart = not isinstance(upper, list)


    def tiles():
        return pl.BlockSpec((rows, TILE), lambda t: (0, t))

    stream_spec = whole((rows, width))
    args = [bits, gain, stream]
    specs = [pl.BlockSpec(memory_space=pltpu.SMEM), whole((1, width)), stream_spec]
    if forward:
        args += stream_parts
        specs += [stream_spec] * 4
    if backward:
        args += [back]
        specs += [stream_spec]
        if not forward:
            args += back_parts + saved
            specs += [stream_spec] * 4 + [tiles()] * 3
    if upper_apart:
        args += [upper] * 4
        specs += [
            pl.BlockSpec((1, 2, 256, TILE), lambda t, i=i: (i, 0, 0, t)) for i in range(4)
        ]
    else:
        args += upper
        specs += [pl.BlockSpec((2, 256, TILE), lambda t: (0, 0, t))] * 4
    args += lower
    specs += [pl.BlockSpec((TILE, 256), lambda t: (t, 0))] * 4
    outs, out_specs = [], []

    def out(shape, dtype, spec=None):
        outs.append(jax.ShapeDtypeStruct(shape, dtype))
        out_specs.append(whole(shape) if spec is None else spec)

    scratch = [pltpu.VMEM((rows, width), BF)]
    if forward:
        out((rows, width), F32)
        out((rows, width), BF)
        scratch += [pltpu.VMEM((rows, width), F32)]
    if backward and not forward:
        out((rows, width), F32)
    if forward and not backward:
        out((rows, hidden), F32, tiles())
        out((rows, hidden), F32, tiles())
        out((rows, hidden), BF, tiles())
    if backward:
        out((rows, 1024 + 3 * hidden), BF)
        out((rows, 512 + 3 * hidden), BF)
        out((rows, 512), BF)
        out((rows, width), BF)
        out((1, width), F32)
        scratch += [pltpu.VMEM((rows, width), BF), pltpu.VMEM((rows, width), F32)]
    flops = rows * width * hidden * 6 * (int(forward) + int(backward))
    return pl.pallas_call(
        functools.partial(ffn_kernel, forward, backward, upper_apart),
        grid=(hidden // TILE,),
        in_specs=specs,
        out_shape=outs,
        out_specs=out_specs,
        scratch_shapes=scratch,
        compiler_params=pltpu.CompilerParams(vmem_limit_bytes=VMEM),
        cost_estimate=pl.CostEstimate(
            flops=flops, bytes_accessed=12 * 2**20, transcendentals=rows * hidden
        ),
    )(*args)


def grads_kernel(tile, upper_steps, own_ref, mine_ref, near_ref, facing_ref, far_ref, out_ref, nt_ref, c_ref):
    step = pl.program_id(0)
    seqs = [(own_ref, 0), (near_ref, 0), (facing_ref, 0), (far_ref, 512)]

    @pl.when(step == 0)
    def _():
        for i, (ref, at) in enumerate(seqs):
            nt_ref[:, i * 128 : (i + 1) * 128] = ref[:, at : at + 256].T
            c_ref[i * 128 : (i + 1) * 128, :] = ref[:, at + 256 : at + 512]

    def columns(ref, start):
        return ref[:, pl.ds(pl.multiple_of(start + step * tile, 128), tile)]

    rows = jnp.concatenate(
        [
            columns(mine_ref, 512),
            columns(near_ref, 512),
            columns(facing_ref, 1024),
            columns(far_ref, 1024),
        ],
        axis=0,
    )

    @pl.when(step < upper_steps)
    def _():
        grad = dot(nt_ref[...], rows).astype(BF)
        for i in range(tile // 128):
            out_ref[i * 256 : (i + 1) * 256, :] = grad[:, i * 128 : (i + 1) * 128]

    @pl.when(step >= upper_steps)
    def _():
        grad = dot(rows.T, c_ref[...]).astype(BF)
        for i in range(2):
            out_ref[i * tile : (i + 1) * tile, :] = grad[:, i * 128 : (i + 1) * 128]


def weight_grads(tile, upper_steps, own, mine, near, facing, far):
    steps = (mine.shape[1] - 512) // tile
    return pl.pallas_call(
        functools.partial(grads_kernel, tile, upper_steps),
        grid=(steps,),
        in_specs=[whole(x.shape) for x in (own, mine, near, facing, far)],
        out_shape=jax.ShapeDtypeStruct((steps * 2 * tile, 128), BF),
        out_specs=pl.BlockSpec((2 * tile, 128), lambda t: (t, 0)),
        scratch_shapes=[pltpu.VMEM((256, 512), BF), pltpu.VMEM((512, 256), BF)],
        compiler_params=pltpu.CompilerParams(vmem_limit_bytes=VMEM),
        cost_estimate=pl.CostEstimate(
            flops=2 * 512 * 256 * steps * tile, bytes_accessed=7 * 2**20, transcendentals=0
        ),
    )(own, mine, near, facing, far)


def unpacked(grads, tile, steps, first):
    part = grads[first * 2 * tile : (first + steps) * 2 * tile]
    return widen(part, steps * tile // 128).astype(F32)


def unpacked_lower(grads, tile, first):
    part = grads[first * 2 * tile : (first + 1) * 2 * tile]
    return widen(part, 2).astype(F32)


def cut_blocks(x):
    return [x[:, i * 256 : (i + 1) * 256] for i in range(4)]


def store_blocks(ref, parts, start=0):
    at = start
    for part in parts:
        ref[:, at : at + part.shape[1]] = part.astype(ref.dtype)
        at += part.shape[1]


def lanes_of(x):
    return lax.broadcasted_iota(jnp.int32, x.shape, 1)


def rows_of(x):
    return lax.broadcasted_iota(jnp.int32, x.shape, 0)


def rotated(u):
    width = u.shape[1]
    first = lanes_of(u) % HD < HD // 2
    return jnp.where(first, -pltpu.roll(u, width - HD // 2, 1), pltpu.roll(u, HD // 2, 1))


def head_means(u):
    lanes = lanes_of(u) // HD
    out = jnp.zeros_like(u)
    for head in range(u.shape[1] // HD):
        mine = lanes == head
        total = jnp.sum(jnp.where(mine, u, 0.0), axis=1, keepdims=True)
        out = jnp.where(mine, total / HD, out)
    return out


def heads_turned(u, gain, cosine, sine):
    scaling = lax.rsqrt(head_means(u * u) + EPS)
    normed = u * scaling
    scaled = normed * gain
    return normed, scaling, scaled * cosine + rotated(scaled) * sine


def heads_back(grad, normed, scaling, gain, cosine, sine):
    du = grad * cosine - rotated(grad * sine)
    gain_grad = jnp.sum(du * normed, axis=0, keepdims=True)
    scaled = du * gain
    return scaling * (scaled - normed * head_means(scaled * normed)), gain_grad


def both_places(x):
    return x.astype(BF), pltpu.roll(x, HD, 1).astype(BF)


def one_head(x, at):
    return jnp.where(lanes_of(x) // HD == at, x, jnp.zeros_like(x))


def side_by_side(left, right):
    return jnp.where(lanes_of(left) < HD, left, right)


def norm_grad(stream, grad, gain, gain_out):
    scaling = scaling_of(stream)
    normed = stream * scaling
    gain_out[...] = jnp.sum(grad * normed, axis=0, keepdims=True)
    grad = grad * gain
    inner = jnp.mean(grad * normed, axis=1, keepdims=True)
    return scaling * (grad - normed * inner)


def store_bundles(ns, cs, wides, facing_out, near_out, own_out):
    store_blocks(own_out, [ns[0], cs[0]])
    store_blocks(near_out, [ns[1], cs[1]] + wides)
    store_blocks(facing_out, [ns[2], cs[2], ns[3], cs[3]] + wides)


def attend_forward_kernel(
    bits_ref, gain_ref, qgain_ref, kgain_ref, cos_ref, sin_ref, base_ref, p0, p1, p2, p3, w0, w1, w2, w3,
    stream_out, partial_out, projected_out, probs_out, att_out,
):
    bits = bits_ref[0]
    weights = (w0, w1, w2, w3)
    stream = plus_parts(base_ref, (p0, p1, p2, p3))
    stream_out[...] = stream
    normed = (stream * scaling_of(stream) * gain_ref[...]).astype(BF)
    projected = jnp.zeros((128, 512), F32)
    for part, weight in zip(kernel_order(cut_blocks(normed), bits), weights):
        projected += dot(part, weight[:, :512])
    projected_out[...] = projected
    cosine, sine = cos_ref[...], sin_ref[...]
    query = heads_turned(projected[:, :256], qgain_ref[...], cosine, sine)[2].astype(BF)
    keys = heads_turned(projected[:, 256:384], kgain_ref[...], cosine[:, :128], sine[:, :128])[2]
    keys = both_places(keys)
    values = both_places(projected[:, 384:])
    causal = rows_of(probs_out[:, :128]) >= lanes_of(probs_out[:, :128])
    for kv in range(2):
        block = query[:, kv * 128 : (kv + 1) * 128]
        mixed = []
        for at in range(2):
            scores = contract_cols(one_head(block, at), keys[at ^ kv]) * HD ** (-0.5)
            scores = jnp.where(causal, scores, MASKED)
            peak = jnp.max(scores, axis=1, keepdims=True)
            logsum = peak + jnp.log(jnp.sum(jnp.exp(scores - peak), axis=1, keepdims=True))
            probs = jnp.exp(scores - logsum)
            head = kv * 2 + at
            probs_out[:, head * 128 : (head + 1) * 128] = probs
            mixed.append(dot(probs.astype(BF), values[at ^ kv]))
        att_out[:, kv * 128 : (kv + 1) * 128] = side_by_side(*mixed).astype(BF)
    att = att_out[...]
    outs = [dot(att, weight[:, 512:]) for weight in weights]
    store_blocks(partial_out, kernel_order(outs, bits))


def attend_backward_kernel(
    bits_ref, gain_ref, qgain_ref, kgain_ref, cos_ref, sin_ref, stream_ref, base_ref, p0, p1, p2, p3,
    projected_ref, probs_ref, att_ref, w0, w1, w2, w3,
    total_out, facing_out, near_out, own_out, back_out, gain_out, qgain_out, kgain_out,
):
    bits = bits_ref[0]
    weights = (w0, w1, w2, w3)
    total = plus_parts(base_ref, (p0, p1, p2, p3))
    total_out[...] = total
    cs = kernel_order(cut_blocks(total.astype(BF)), bits)
    grad = jnp.zeros((128, 256), F32)
    for part, weight in zip(cs, weights):
        grad += contract_cols(part, weight[:, 512:])
    grad = grad.astype(BF)
    cosine, sine = cos_ref[...], sin_ref[...]
    projected = projected_ref[...]
    qnormed, qscaling, query = heads_turned(projected[:, :256], qgain_ref[...], cosine, sine)
    query = query.astype(BF)
    knormed, kscaling, keys = heads_turned(
        projected[:, 256:384], kgain_ref[...], cosine[:, :128], sine[:, :128]
    )
    keys = both_places(keys)
    values = both_places(projected[:, 384:])
    dquery, dkeys, dvalues = [], [], []
    for kv in range(2):
        block = query[:, kv * 128 : (kv + 1) * 128]
        gblock = grad[:, kv * 128 : (kv + 1) * 128]
        dqs = []
        dk = jnp.zeros((128, 128), F32)
        dv = jnp.zeros((128, 128), F32)
        for at in range(2):
            head = kv * 2 + at
            probs = probs_ref[:, head * 128 : (head + 1) * 128]
            mine = one_head(gblock, at)
            dv += dot(probs.T.astype(BF), mine)
            dprobs = contract_cols(mine, values[at ^ kv])
            delta = jnp.sum(probs * dprobs, axis=1, keepdims=True)
            dscores = probs * (dprobs - delta)
            dqs.append(dot(dscores.astype(BF), keys[at ^ kv]))
            dk += dot(dscores.T.astype(BF), one_head(block, at))
        dquery.append(side_by_side(*dqs) * HD ** (-0.5))
        dkeys.append((dk + pltpu.roll(dk, HD, 1)) * HD ** (-0.5))
        dvalues.append(dv + pltpu.roll(dv, HD, 1))
    dquery = jnp.concatenate(dquery, axis=1)
    dquery, qgain = heads_back(dquery, qnormed, qscaling, qgain_ref[...], cosine, sine)
    dkeys, kgain = heads_back(
        side_by_side(*dkeys), knormed, kscaling, kgain_ref[...], cosine[:, :128], sine[:, :128]
    )
    qgain_out[...] = qgain
    kgain_out[...] = kgain
    pieces = jnp.concatenate([dquery, dkeys, side_by_side(*dvalues)], axis=1).astype(BF)
    outs = [contract_cols(pieces, weight[:, :512]) for weight in weights]
    grad = jnp.concatenate(kernel_order(outs, bits), axis=1)
    stream = stream_ref[...]
    back_out[...] = norm_grad(stream, grad, gain_ref[...], gain_out).astype(BF)
    normed = (stream * scaling_of(stream) * gain_ref[...]).astype(BF)
    ns = kernel_order(cut_blocks(normed), bits)
    store_bundles(ns, cs, [pieces, att_ref[...]], facing_out, near_out, own_out)


def shifted_down(x, count):
    if count == 0:
        return x
    return jnp.where(rows_of(x) >= count, pltpu.roll(x, count, 0), 0.0)


def shifted_up(x, count):
    if count == 0:
        return x
    rows = x.shape[0]
    return jnp.where(rows_of(x) < rows - count, pltpu.roll(x, rows - count, 0), 0.0)


def mixer_weights(own_in, core_in, low, high, core_low, core_high, own_out, core_out):
    ins = [
        [own_in[k], core_in[k], (low, high)[k // 2][k % 2], (core_low, core_high)[k // 2][k % 2]]
        for k in range(3)
    ]
    return ins, [own_out[...], core_out[...], high[1], core_high[1]]


def convolved(bx, taps_ref):
    return sum(shifted_down(bx, KW - 1 - k) * taps_ref[k : k + 1, :] for k in range(KW))


def mixer_forward_kernel(bits_ref, gain_ref, taps_ref, stream_ref, *refs):
    ins, outs = mixer_weights(*refs[:8])
    partial_out, projected_out, mix_out = refs[8:]
    bits = bits_ref[0]
    stream = stream_ref[...]
    normed = (stream * scaling_of(stream) * gain_ref[...]).astype(BF)
    ns = kernel_order(cut_blocks(normed), bits)
    projected = []
    for k in range(3):
        total = jnp.zeros((128, 256), F32)
        for part, weight in zip(ns, ins[k]):
            total += dot(part, weight)
        projected.append(total)
        projected_out[k] = total
    mix = (projected[1] * convolved(projected[0] * projected[2], taps_ref)).astype(BF)
    mix_out[...] = mix
    store_blocks(partial_out, kernel_order([dot(mix, weight) for weight in outs], bits))


def mixer_backward_kernel(
    bits_ref, gain_ref, taps_ref, stream_ref, base_ref, p0, p1, p2, p3, start_ref, projected_ref, mix_ref, *refs
):
    ins, outs = mixer_weights(*refs[:8])
    facing_out, near_out, own_out, back_out, gain_out, taps_out = refs[8:]
    bits = bits_ref[0]
    total = plus_parts(base_ref, (p0, p1, p2, p3))
    cs = kernel_order(cut_blocks(total.astype(BF)), bits)
    dmix = jnp.zeros((128, 256), F32)
    for part, weight in zip(cs, outs):
        dmix += contract_cols(part, weight)
    pb, pc, px = projected_ref[0], projected_ref[1], projected_ref[2]
    bx = pb * px
    dconv = dmix * pc
    for k in range(KW):
        taps_out[k : k + 1, :] = jnp.sum(
            dconv * shifted_down(bx, KW - 1 - k), axis=0, keepdims=True
        )
    dbx = sum(shifted_up(dconv, KW - 1 - k) * taps_ref[k : k + 1, :] for k in range(KW))
    pieces = [
        (dbx * px).astype(BF),
        (dmix * convolved(bx, taps_ref)).astype(BF),
        (dbx * pb).astype(BF),
    ]
    grads = []
    for i in range(4):
        grads.append(sum(contract_cols(pieces[k], ins[k][i]) for k in range(3)))
    grad = jnp.concatenate(kernel_order(grads, bits), axis=1)
    stream = stream_ref[...]
    back = norm_grad(stream, grad, gain_ref[...], gain_out) + 0.25 * (total - start_ref[...])
    store_blocks(back_out, kernel_order(cut_blocks(back.astype(BF)), bits_ref[1]))
    normed = (stream * scaling_of(stream) * gain_ref[...]).astype(BF)
    ns = kernel_order(cut_blocks(normed), bits)
    store_bundles(ns, cs, pieces + [mix_ref[...]], facing_out, near_out, own_out)


def in_one_step(kernel, args, outs, flops):
    return pl.pallas_call(
        kernel,
        grid=(1,),
        in_specs=[pl.BlockSpec(memory_space=pltpu.SMEM)] + [whole(x.shape) for x in args[1:]],
        out_shape=[jax.ShapeDtypeStruct(shape, dtype) for shape, dtype in outs],
        out_specs=[whole(shape) for shape, dtype in outs],
        compiler_params=pltpu.CompilerParams(vmem_limit_bytes=VMEM),
        cost_estimate=pl.CostEstimate(
            flops=flops, bytes_accessed=6 * 2**20, transcendentals=128 * 1024
        ),
    )(*args)


def tied(*values):
    return lax.optimization_barrier(values)


def unpack_kernel(in_ref, upper_out, lower_out):
    for k in range(2):
        for i in range(9):
            at = (k * 9 + i) * 256
            upper_out[k, :, i * 128 : (i + 1) * 128] = in_ref[at : at + 256, :].astype(F32)
    for i in range(3):
        for half in range(2):
            at = 18 * 256 + (i * 2 + half) * TILE
            lower_out[i * TILE : (i + 1) * TILE, half * 128 : (half + 1) * 128] = in_ref[
                at : at + TILE, :
            ].astype(F32)


def ffn_unpacked(grads):
    shapes = [(2, 256, 3 * TILE), (3 * TILE, 256)]
    return pl.pallas_call(
        unpack_kernel,
        grid=(1,),
        in_specs=[whole(grads.shape)],
        out_shape=[jax.ShapeDtypeStruct(shape, F32) for shape in shapes],
        out_specs=[whole(shape) for shape in shapes],
        compiler_params=pltpu.CompilerParams(vmem_limit_bytes=VMEM),
    )(grads)


def scattered_z(g):
    return lax.psum_scatter(g, "z", scatter_dimension=0, tiled=True)


def plus_xl(part):
    return (part.astype(F32) + from_xl(part).astype(F32)).astype(BF)


def gathered_z_directly(piece):
    pieces = [piece] + [from_z(piece, bits) for bits in (1, 2, 3)]
    return jnp.concatenate(xor_order(pieces, lax.axis_index("z")), axis=0)


def gathered_z(part):
    return lax.all_gather(part, "z", axis=0, tiled=True)


def body(
    stream_in,
    cotangent,
    mixer_gain,
    mixer_input,
    mixer_kernel,
    mixer_output,
    front_gain,
    front_upper,
    front_lower,
    attend_gain,
    attend_query,
    attend_keyval,
    query_gain,
    key_gain,
    attend_output,
    rear_gain,
    rear_upper,
    rear_lower,
):
    bits = place()[0].astype(jnp.int32).reshape(1)
    x, cot = spread_in([stream_in, cotangent])
    even = lax.axis_index("xl") == 0
    mixer_got = from_facing(
        jnp.where(
            even,
            mixer_input[:2],
            jnp.concatenate([mixer_input[2:], mixer_output[None]], axis=0),
        )
    )
    x, mixer_got, gains, front_upper, front_lower = tied(
        x,
        mixer_got,
        jnp.stack([mixer_gain, front_gain, attend_gain, rear_gain]),
        front_upper,
        front_lower,
    )
    gains = whole_order(gathered(gains))
    mixer_other = from_xl(mixer_got)
    fu = front_upper
    fu_got = facing_half(fu)
    fl_facing = from_facing(front_lower)
    low = jnp.where(even, mixer_other, mixer_got)
    high = jnp.where(even, mixer_got, mixer_other)
    core_input, core_output = from_core(mixer_input), from_core(mixer_output)
    core_low, core_high = from_core(low), from_core(high)
    mixer = [mixer_input, core_input, low, high, core_low, core_high, mixer_output, core_output]
    attend = jnp.concatenate(
        [attend_query, attend_keyval[0], attend_keyval[1], attend_output], axis=1
    )
    tokens, width = x.shape
    wide = (tokens, width)
    cosine, sine = rope_tables(tokens)
    tables = [
        gains[2:3],
        jnp.tile(query_gain, 4)[None],
        jnp.tile(key_gain, 2)[None],
        jnp.tile(cosine[:, 0], (1, 4)),
        jnp.tile(sine[:, 0], (1, 4)),
    ]
    partial, projected, mixes = in_one_step(
        mixer_forward_kernel,
        [bits, gains[:1], mixer_kernel, x] + mixer,
        [(wide, BF), ((3, tokens, 256), F32), ((tokens, 256), BF)],
        2 * tokens * width * 1024,
    )
    partial, fu_got = tied(partial, fu_got)
    parts = over_y(partial)
    fu_other = from_xl(fu_got)
    parts, fu_other, fl_facing, attend = tied(parts, fu_other, fl_facing, attend)
    attend_facing = from_facing(attend)
    fu = with_facing(fu, fu_got, fu_other)
    fl = [front_lower, from_core(front_lower), fl_facing, from_core(fl_facing)]
    first, partial, *front_saved = ffn(
        True, False, bits, gains[1:2], x, parts, None, None, None, fu, fl
    )
    partial, attend_facing, rear_upper = tied(partial, attend_facing, rear_upper)
    attend = [attend, from_core(attend), attend_facing, from_core(attend_facing)]
    ru = gathered_apart(rear_upper)
    parts, rear_lower = tied(over_y(partial), rear_lower)
    rl_facing = from_facing(rear_lower)
    second, partial, attn_projected, probs, attended = in_one_step(
        attend_forward_kernel,
        [bits] + tables + [first] + parts + attend,
        [
            (wide, F32),
            (wide, BF),
            ((tokens, 512), F32),
            ((tokens, 512), F32),
            ((tokens, 256), BF),
        ],
        2 * tokens * width * 1024,
    )
    parts, rl_facing = tied(over_y(partial), rl_facing)
    rl = [rear_lower, from_core(rear_lower), rl_facing, from_core(rl_facing)]
    third, partial, facing_bundle, near_bundle, own, back, rear_gain_grad = ffn(
        True, True, bits, gains[3:4], second, parts, cot, None, None, ru, rl
    )
    sent_out = jnp.concatenate(
        xor_order(blocks((partial.astype(F32) + 0.25 * (third - x)).astype(BF)), place()[1]), axis=1
    )
    rear_near = from_core(near_bundle)
    back_parts, facing_bundle = tied(over_y(back), facing_bundle)
    rear_facing = from_facing(facing_bundle)
    rear_mine, rear_own = near_bundle, own
    (
        third_grad,
        attn_facing,
        attn_mine,
        attn_own,
        sent,
        attend_gain_grad,
        qgain_grad,
        kgain_grad,
    ) = in_one_step(
        attend_backward_kernel,
        [bits] + tables + [second, cot] + back_parts + [attn_projected, probs, attended] + attend,
        [
            (wide, F32),
            ((tokens, 1792), BF),
            ((tokens, 1280), BF),
            ((tokens, 512), BF),
            (wide, BF),
            ((1, width), F32),
            ((1, 256), F32),
            ((1, 128), F32),
        ],
        4 * tokens * width * 1024,
    )
    qgain_grad = jnp.sum(qgain_grad.reshape(4, HD), axis=0)
    kgain_grad = jnp.sum(kgain_grad.reshape(2, HD), axis=0)
    parts, rear_facing, rear_near, attn_facing, attn_mine = tied(
        over_y(sent), rear_facing, rear_near, attn_facing, attn_mine
    )
    attn_facing = from_facing(attn_facing)
    rear_far = from_core(rear_facing)
    second_grad, facing_bundle, near_bundle, own, back, front_gain_grad = ffn(
        False, True, bits, gains[1:2], first, None, third_grad, parts, front_saved, fu, fl
    )
    back, rear_far, attn_facing = tied(back, rear_far, attn_facing)
    parts = over_y(back)
    front_facing = from_facing(facing_bundle)
    rear_grads = weight_grads(TILE, 6, rear_own, rear_mine, rear_near, rear_facing, rear_far)
    rear_part = scattered_z(rear_grads)
    parts, rear_grads, near_bundle, attn_mine = tied(parts, rear_grads, near_bundle, attn_mine)
    front_near = from_core(near_bundle)
    attn_near = from_core(attn_mine)
    mixer_facing, mixer_mine, mixer_own, stream_back, mixer_gain_grad, kernel_grad = in_one_step(
        mixer_backward_kernel,
        [jnp.stack(place()).astype(jnp.int32), gains[:1], mixer_kernel, x, second_grad]
        + parts
        + [cot, projected, mixes]
        + mixer,
        [
            ((tokens, 2048), BF),
            ((tokens, 1536), BF),
            ((tokens, 512), BF),
            (wide, BF),
            ((1, width), F32),
            ((KW, 256), F32),
        ],
        4 * tokens * width * 1024,
    )
    own, stream_back, mixer_facing, mixer_mine, rear_part = tied(
        own, stream_back, mixer_facing, mixer_mine, rear_part
    )
    mixer_near = from_core(mixer_mine)
    mixer_facing = from_facing(mixer_facing)
    rear_part = plus_xl(rear_part)
    gain_rows = jnp.concatenate(
        [mixer_gain_grad, front_gain_grad, attend_gain_grad, rear_gain_grad], axis=0
    )
    head_row = jnp.pad(jnp.concatenate([qgain_grad, kgain_grad]), (0, width - 2 * HD))[None]
    rows = jnp.concatenate([gain_rows, head_row], axis=0)
    rows = rows + from_y(rows, 1) + from_y(rows, 2) + from_y(rows, 3)
    own_row, near_row, far_row, last_row = own_order(rows[:4])
    others = jnp.concatenate([kernel_grad, rows[4:, :256]], axis=0)
    got = from_core(jnp.concatenate([near_row, last_row, others], axis=0))
    rows = jnp.concatenate([own_row, far_row, others], axis=0) + got
    rows = jnp.concatenate([rows[:4], rows[8:]], axis=0) + from_facing(rows[4:])
    rows = jnp.pad(jnp.concatenate([rows[:, :128], rows[:, 128:]], axis=0), ((0, 48), (0, 0)))

    front_grads = weight_grads(
        TILE, 6, own, near_bundle, front_near, front_facing, from_core(front_facing)
    )
    front_part = scattered_z(front_grads)
    front_grads, mixer_facing, rear_part = tied(front_grads, mixer_facing, rear_part)
    attn_grads = weight_grads(
        256, 2, attn_own, attn_mine, attn_near, attn_facing, from_core(attn_facing)
    )
    mixer_grads = weight_grads(
        256, 3, mixer_own, mixer_mine, mixer_near, mixer_facing, from_core(mixer_facing)
    )
    rear_all = gathered_z(rear_part)
    bundle, front_part = tied(
        jnp.concatenate([mixer_grads, attn_grads, rows.astype(BF)], axis=0), front_part
    )
    front_part = plus_xl(front_part)
    sent = dp_sum_begun(bundle)
    sent, front_part, stream_back, sent_out = tied(sent, front_part, stream_back, sent_out)
    sum_back, sum_out = bring_back([stream_back, sent_out])
    stream_grad = cotangent + sum_back
    fourth = stream_in + sum_out
    small_grads = dp_sum_ended(sent)
    front_all = gathered_z(front_part)
    rear_upper_grad, rear_lower_grad = ffn_unpacked(rear_all)
    rear_upper_grad, rear_lower_grad, small_grads, stream_grad, fourth, front_all = tied(
        rear_upper_grad, rear_lower_grad, small_grads, stream_grad, fourth, front_all
    )
    cut = mixer_grads.shape[0]
    mixer_grads, attn_grads = small_grads[:cut], small_grads[cut : cut + attn_grads.shape[0]]
    rows = small_grads[-64:-48].astype(F32)
    sums = jnp.concatenate([rows[:8], rows[8:]], axis=1)
    input_grad = jnp.stack([unpacked(mixer_grads, 256, 1, k) for k in range(3)])
    mixer_output_grad = unpacked_lower(mixer_grads, 256, 3)
    attend_query_grad = unpacked(attn_grads, 256, 1, 0)
    keyval_grad = attn_grads[512:1024].astype(F32).reshape(2, 256, 128)
    attend_output_grad = unpacked_lower(attn_grads, 256, 2)
    front_upper_grad, front_lower_grad = ffn_unpacked(front_all)
    return (
        fourth,
        stream_grad,
        sums[0],
        input_grad,
        sums[4:7],
        mixer_output_grad,
        sums[1],
        front_upper_grad,
        front_lower_grad,
        sums[2],
        attend_query_grad,
        keyval_grad,
        sums[7, :HD],
        sums[7, HD : 2 * HD],
        attend_output_grad,
        sums[3],
        rear_upper_grad,
        rear_lower_grad,
    )


def solution(mesh):
    parts = Mesh(mesh.devices.reshape(4, 2, 2, 2, 4), ("z", "xl", "xh", "core", "y"))
    tokens = ("z", "xl", "y")
    row = ("xh", "core")
    stream = P(tokens, row)
    gain = P(row)
    upper = P(None, row, "y")
    lower = P("y", row)
    weights = (
        gain,
        upper,
        P(None, "y"),
        lower,
        gain,
        upper,
        lower,
        gain,
        P(row, "y"),
        upper,
        P(),
        P(),
        lower,
        gain,
        upper,
        lower,
    )
    return jax.shard_map(
        body,
        mesh=parts,
        in_specs=(stream, stream) + weights,
        out_specs=(stream, stream) + weights,
        check_vma=False,
    )
```

```python
import functools

import jax
import jax.numpy as jnp
from jax import lax
from jax.experimental import pallas as pl
from jax.experimental.pallas import tpu as pltpu
from jax.sharding import Mesh
from jax.sharding import PartitionSpec as P

D = 1024
HD = 64
KW = 3


EPS = 1e-05
THETA = 1000000.0
MASKED = -1e30

def contract_cols(left, right):
    return lax.dot_general(
        left, right, (((1,), (1,)), ((), ())), preferred_element_type=jnp.float32
    )


def rope_tables(length):
    half = HD // 2
    freqs = jnp.power(THETA, -(jnp.arange(half, dtype=jnp.float32) * 2.0 / HD))
    angles = jnp.arange(length, dtype=jnp.float32)[:, None] * freqs[None, :]
    cosine = jnp.concatenate([jnp.cos(angles), jnp.cos(angles)], axis=1)[:, None, :]
    sine = jnp.concatenate([jnp.sin(angles), jnp.sin(angles)], axis=1)[:, None, :]
    return (cosine, sine)


BF = jnp.bfloat16
F32 = jnp.float32


def xor_pairs(count, bits):
    return [(i, i ^ bits) for i in range(count)]


def from_core(x):
    return lax.ppermute(x, "core", xor_pairs(2, 1))


def from_facing(x):
    return lax.ppermute(x, ("xl", "xh"), xor_pairs(4, 3))


def from_xl(x):
    return lax.ppermute(x, "xl", xor_pairs(2, 1))


def from_z(x, bits):
    return lax.ppermute(x, "z", xor_pairs(4, bits))


def from_y(x, bits):
    return lax.ppermute(x, "y", xor_pairs(4, bits))


def gathered(shard):
    facing = from_facing(shard)
    others = from_core(jnp.stack([shard, facing]))
    return [shard, others[0], facing, others[1]]


def facing_half(halves):
    return from_facing(lax.dynamic_index_in_dim(halves, lax.axis_index("xl"), 0, keepdims=False))


def with_facing(halves, got, other):
    first = lax.axis_index("xl") == 0
    facing = jnp.stack([jnp.where(first, other, got), jnp.where(first, got, other)])
    return [halves, from_core(halves), facing, from_core(facing)]


def gathered_apart(shard):
    return lax.all_gather(shard, ("xh", "core"), axis=0, tiled=False)


def over_y(sent):
    return [sent] + [from_y(sent, bits) for bits in (1, 3, 2)]


def summed_y(x):
    return sum(part.astype(F32) for part in over_y(x.astype(BF)))


def blocks(x):
    width = x.shape[1] // 4
    return [x[:, i * width : (i + 1) * width] for i in range(4)]


def xor_order(parts, index):
    low = (index & 1) == 1
    high = (index & 2) == 2
    a = [jnp.where(low, parts[i ^ 1], parts[i]) for i in range(4)]
    return [jnp.where(high, a[i ^ 2], a[i]) for i in range(4)]


def place():
    return lax.axis_index("xh") * 2 + lax.axis_index("core"), lax.axis_index("y")


def own_order(x):
    return xor_order(blocks(x), place()[0])


def whole_order(parts):
    return jnp.concatenate(xor_order(parts, place()[0]), axis=1)


def spread_in(arrays):
    col = place()[1]
    x = jnp.concatenate(arrays, axis=1).astype(BF)
    parts = []
    for bits in range(4):
        pairs = [(w * 4 + s, s * 4 + (w ^ bits)) for w in range(4) for s in range(4)]
        parts.append(lax.ppermute(x, ("xh", "core", "y"), pairs))
    parts = xor_order(parts, col)
    return [
        jnp.concatenate([part[:, i * 256 : (i + 1) * 256] for part in parts], axis=1).astype(F32)
        for i in range(len(arrays))
    ]


def bring_back(arrays):
    parts = [jnp.concatenate(at, axis=1) for at in zip(*[blocks(x) for x in arrays])]
    total = None
    for bits in range(4):
        pairs = [(s * 4 + c, (c ^ bits) * 4 + s) for s in range(4) for c in range(4)]
        got = lax.ppermute(parts[bits], ("xh", "core", "y"), pairs).astype(F32)
        total = got if total is None else total + got
    return [total[:, i * 256 : (i + 1) * 256] for i in range(len(arrays))]


def widen(x, count):
    rows = x.shape[0] // count
    return jnp.concatenate([x[i * rows : (i + 1) * rows] for i in range(count)], axis=1)


def dp_sum_begun(g):
    z = lax.axis_index("z")
    g = g.astype(BF)
    quarter = g.shape[0] // 4

    def chunk(at):
        return lax.dynamic_slice_in_dim(g, at * quarter, quarter, 0)

    total = chunk(z).astype(F32)
    for bits in (1, 3, 2):
        total = total + from_z(chunk(z ^ bits), bits).astype(F32)
    return total.astype(BF)


def dp_sum_ended(sent):
    return gathered_z_directly(plus_xl(sent))


def dot(left, right):
    return jnp.dot(left, right, preferred_element_type=F32)


TILE = 384
VMEM = 56 * 2**20


def kernel_order(parts, bits):
    low = (bits & 1) == 1
    high = (bits & 2) == 2
    a = [jnp.where(low, parts[i ^ 1], parts[i]) for i in range(4)]
    return [jnp.where(high, a[i ^ 2], a[i]) for i in range(4)]


def plus_parts(base_ref, part_refs):
    total = base_ref[...]
    for ref in part_refs:
        total = total + ref[...].astype(F32)
    return total


def scaling_of(values):
    return lax.rsqrt(jnp.mean(values * values, axis=1, keepdims=True) + EPS)


def ffn_kernel(forward, backward, upper_apart, *refs):
    refs = list(refs)

    def take(count):
        out = refs[:count]
        del refs[:count]
        return out

    bits = refs.pop(0)[0]
    gain_ref = refs.pop(0)
    stream_ref = refs.pop(0)
    stream_parts = take(4) if forward else []
    if backward:
        back_ref = refs.pop(0)
        back_parts = [] if forward else take(4)
    if backward and not forward:
        gating_in, upward_in, hidden_in = take(3)
    uppers = take(4)
    lowers = take(4)
    if forward:
        stream_out, partial_out = take(2)
    if backward and not forward:
        total_out = refs.pop(0)
    if forward and not backward:
        gating_out, upward_out, hidden_out = take(3)
    if backward:
        facing_out, near_out, own_out, back_out, gain_out = take(5)
    n_ref = refs.pop(0)
    if forward:
        down_ref = refs.pop(0)
    if backward:
        c_ref, grad_ref = take(2)
    step = pl.program_id(0)
    last = pl.num_programs(0) - 1

    def cut(x):
        return [x[:, i * 256 : (i + 1) * 256] for i in range(4)]

    def upper(i, member):
        return uppers[i][0, member] if upper_apart else uppers[i][member]

    def apart(parts):
        return parts if upper_apart else kernel_order(parts, bits)

    @pl.when(step == 0)
    def _():
        if forward:
            stream = plus_parts(stream_ref, stream_parts)
            stream_out[...] = stream
        else:
            stream = stream_ref[...]
        normed = (stream * scaling_of(stream) * gain_ref[...]).astype(BF)
        if forward:
            for i, part in enumerate(apart(cut(normed))):
                n_ref[:, i * 256 : (i + 1) * 256] = part
            down_ref[...] = jnp.zeros_like(down_ref)
        if backward:
            upstream = plus_parts(back_ref, back_parts)
            if not forward:
                total_out[...] = upstream
            cs = kernel_order(cut(upstream.astype(BF)), bits)
            ns = kernel_order(cut(normed), bits)
            for i in range(4):
                c_ref[:, i * 256 : (i + 1) * 256] = cs[i]
            grad_ref[...] = jnp.zeros_like(grad_ref)
            own_out[:, :256] = ns[0]
            own_out[:, 256:] = cs[0]
            near_out[:, :256] = ns[1]
            near_out[:, 256:512] = cs[1]
            for i in (2, 3):
                facing_out[:, (i - 2) * 512 : (i - 2) * 512 + 256] = ns[i]
                facing_out[:, (i - 2) * 512 + 256 : (i - 1) * 512] = cs[i]

    if forward:
        gating = jnp.zeros((n_ref.shape[0], TILE), F32)
        upward = gating
        for i, part in enumerate(cut(n_ref)):
            gating += dot(part, upper(i, 0))
            upward += dot(part, upper(i, 1))
        hidden = (gating * jax.nn.sigmoid(gating) * upward).astype(BF)
        for i in range(4):
            down_ref[:, i * 256 : (i + 1) * 256] += dot(hidden, lowers[i][...])
        if not backward:
            gating_out[...] = gating
            upward_out[...] = upward
            hidden_out[...] = hidden

        @pl.when(step == last)
        def _():
            for i, part in enumerate(kernel_order(cut(down_ref), bits)):
                partial_out[:, i * 256 : (i + 1) * 256] = part.astype(BF)

    if backward:
        if not forward:
            gating, upward, hidden = gating_in[...], upward_in[...], hidden_in[...]
        hidden_grad = jnp.zeros((c_ref.shape[0], TILE), F32)
        for i, part in enumerate(cut(c_ref)):
            hidden_grad += contract_cols(part, lowers[i][...])
        sigmoid = jax.nn.sigmoid(gating)
        gating_grad = (hidden_grad * upward * sigmoid * (1.0 + gating * (1.0 - sigmoid))).astype(BF)
        upward_grad = (hidden_grad * gating * sigmoid).astype(BF)
        for i in range(4):
            grad_ref[:, i * 256 : (i + 1) * 256] += contract_cols(
                gating_grad, upper(i, 0)
            ) + contract_cols(upward_grad, upper(i, 1))
        for at, piece in enumerate((gating_grad, upward_grad, hidden)):
            place_at = at * 1152 + step * TILE
            near_out[:, pl.ds(pl.multiple_of(512 + place_at, 128), TILE)] = piece
            facing_out[:, pl.ds(pl.multiple_of(1024 + place_at, 128), TILE)] = piece

        @pl.when(step == last)
        def _():
            stream = stream_out[...] if forward else stream_ref[...]
            scaling = scaling_of(stream)
            normed = stream * scaling
            grad = jnp.concatenate(apart(cut(grad_ref)), axis=1)
            gain_out[...] = jnp.sum(grad * normed, axis=0, keepdims=True)
            grad = grad * gain_ref[...]
            inner = jnp.mean(grad * normed, axis=1, keepdims=True)
            back_out[...] = (scaling * (grad - normed * inner)).astype(BF)


def whole(shape):
    return pl.BlockSpec(shape, lambda *_: (0,) * len(shape))


def ffn(forward, backward, bits, gain, stream, stream_parts, back, back_parts, saved, upper, lower):
    rows, width = stream.shape
    hidden = lower[0].shape[0]
    upper_apart = not isinstance(upper, list)


    def tiles():
        return pl.BlockSpec((rows, TILE), lambda t: (0, t))

    stream_spec = whole((rows, width))
    args = [bits, gain, stream]
    specs = [pl.BlockSpec(memory_space=pltpu.SMEM), whole((1, width)), stream_spec]
    if forward:
        args += stream_parts
        specs += [stream_spec] * 4
    if backward:
        args += [back]
        specs += [stream_spec]
        if not forward:
            args += back_parts + saved
            specs += [stream_spec] * 4 + [tiles()] * 3
    if upper_apart:
        args += [upper] * 4
        specs += [
            pl.BlockSpec((1, 2, 256, TILE), lambda t, i=i: (i, 0, 0, t)) for i in range(4)
        ]
    else:
        args += upper
        specs += [pl.BlockSpec((2, 256, TILE), lambda t: (0, 0, t))] * 4
    args += lower
    specs += [pl.BlockSpec((TILE, 256), lambda t: (t, 0))] * 4
    outs, out_specs = [], []

    def out(shape, dtype, spec=None):
        outs.append(jax.ShapeDtypeStruct(shape, dtype))
        out_specs.append(whole(shape) if spec is None else spec)

    scratch = [pltpu.VMEM((rows, width), BF)]
    if forward:
        out((rows, width), F32)
        out((rows, width), BF)
        scratch += [pltpu.VMEM((rows, width), F32)]
    if backward and not forward:
        out((rows, width), F32)
    if forward and not backward:
        out((rows, hidden), F32, tiles())
        out((rows, hidden), F32, tiles())
        out((rows, hidden), BF, tiles())
    if backward:
        out((rows, 1024 + 3 * hidden), BF)
        out((rows, 512 + 3 * hidden), BF)
        out((rows, 512), BF)
        out((rows, width), BF)
        out((1, width), F32)
        scratch += [pltpu.VMEM((rows, width), BF), pltpu.VMEM((rows, width), F32)]
    flops = rows * width * hidden * 6 * (int(forward) + int(backward))
    return pl.pallas_call(
        functools.partial(ffn_kernel, forward, backward, upper_apart),
        grid=(hidden // TILE,),
        in_specs=specs,
        out_shape=outs,
        out_specs=out_specs,
        scratch_shapes=scratch,
        compiler_params=pltpu.CompilerParams(vmem_limit_bytes=VMEM),
        cost_estimate=pl.CostEstimate(
            flops=flops, bytes_accessed=12 * 2**20, transcendentals=rows * hidden
        ),
    )(*args)


def grads_kernel(tile, upper_steps, own_ref, mine_ref, near_ref, facing_ref, far_ref, out_ref, nt_ref, c_ref):
    step = pl.program_id(0)
    seqs = [(own_ref, 0), (near_ref, 0), (facing_ref, 0), (far_ref, 512)]

    @pl.when(step == 0)
    def _():
        for i, (ref, at) in enumerate(seqs):
            nt_ref[:, i * 128 : (i + 1) * 128] = ref[:, at : at + 256].T
            c_ref[i * 128 : (i + 1) * 128, :] = ref[:, at + 256 : at + 512]

    def columns(ref, start):
        return ref[:, pl.ds(pl.multiple_of(start + step * tile, 128), tile)]

    rows = jnp.concatenate(
        [
            columns(mine_ref, 512),
            columns(near_ref, 512),
            columns(facing_ref, 1024),
            columns(far_ref, 1024),
        ],
        axis=0,
    )

    @pl.when(step < upper_steps)
    def _():
        grad = dot(nt_ref[...], rows).astype(BF)
        for i in range(tile // 128):
            out_ref[i * 256 : (i + 1) * 256, :] = grad[:, i * 128 : (i + 1) * 128]

    @pl.when(step >= upper_steps)
    def _():
        grad = dot(rows.T, c_ref[...]).astype(BF)
        for i in range(2):
            out_ref[i * tile : (i + 1) * tile, :] = grad[:, i * 128 : (i + 1) * 128]


def weight_grads(tile, upper_steps, own, mine, near, facing, far):
    steps = (mine.shape[1] - 512) // tile
    return pl.pallas_call(
        functools.partial(grads_kernel, tile, upper_steps),
        grid=(steps,),
        in_specs=[whole(x.shape) for x in (own, mine, near, facing, far)],
        out_shape=jax.ShapeDtypeStruct((steps * 2 * tile, 128), BF),
        out_specs=pl.BlockSpec((2 * tile, 128), lambda t: (t, 0)),
        scratch_shapes=[pltpu.VMEM((256, 512), BF), pltpu.VMEM((512, 256), BF)],
        compiler_params=pltpu.CompilerParams(vmem_limit_bytes=VMEM),
        cost_estimate=pl.CostEstimate(
            flops=2 * 512 * 256 * steps * tile, bytes_accessed=7 * 2**20, transcendentals=0
        ),
    )(own, mine, near, facing, far)


def unpacked(grads, tile, steps, first):
    part = grads[first * 2 * tile : (first + steps) * 2 * tile]
    return widen(part, steps * tile // 128).astype(F32)


def unpacked_lower(grads, tile, first):
    part = grads[first * 2 * tile : (first + 1) * 2 * tile]
    return widen(part, 2).astype(F32)


def cut_blocks(x):
    return [x[:, i * 256 : (i + 1) * 256] for i in range(4)]


def store_blocks(ref, parts, start=0):
    at = start
    for part in parts:
        ref[:, at : at + part.shape[1]] = part.astype(ref.dtype)
        at += part.shape[1]


def lanes_of(x):
    return lax.broadcasted_iota(jnp.int32, x.shape, 1)


def rows_of(x):
    return lax.broadcasted_iota(jnp.int32, x.shape, 0)


def rotated(u):
    width = u.shape[1]
    first = lanes_of(u) % HD < HD // 2
    return jnp.where(first, -pltpu.roll(u, width - HD // 2, 1), pltpu.roll(u, HD // 2, 1))


def head_means(u):
    lanes = lanes_of(u) // HD
    out = jnp.zeros_like(u)
    for head in range(u.shape[1] // HD):
        mine = lanes == head
        total = jnp.sum(jnp.where(mine, u, 0.0), axis=1, keepdims=True)
        out = jnp.where(mine, total / HD, out)
    return out


def heads_turned(u, gain, cosine, sine):
    scaling = lax.rsqrt(head_means(u * u) + EPS)
    normed = u * scaling
    scaled = normed * gain
    return normed, scaling, scaled * cosine + rotated(scaled) * sine


def heads_back(grad, normed, scaling, gain, cosine, sine):
    du = grad * cosine - rotated(grad * sine)
    gain_grad = jnp.sum(du * normed, axis=0, keepdims=True)
    scaled = du * gain
    return scaling * (scaled - normed * head_means(scaled * normed)), gain_grad


def both_places(x):
    return x.astype(BF), pltpu.roll(x, HD, 1).astype(BF)


def one_head(x, at):
    return jnp.where(lanes_of(x) // HD == at, x, jnp.zeros_like(x))


def side_by_side(left, right):
    return jnp.where(lanes_of(left) < HD, left, right)


def norm_grad(stream, grad, gain, gain_out):
    scaling = scaling_of(stream)
    normed = stream * scaling
    gain_out[...] = jnp.sum(grad * normed, axis=0, keepdims=True)
    grad = grad * gain
    inner = jnp.mean(grad * normed, axis=1, keepdims=True)
    return scaling * (grad - normed * inner)


def store_bundles(ns, cs, wides, facing_out, near_out, own_out):
    store_blocks(own_out, [ns[0], cs[0]])
    store_blocks(near_out, [ns[1], cs[1]] + wides)
    store_blocks(facing_out, [ns[2], cs[2], ns[3], cs[3]] + wides)


def attend_forward_kernel(
    bits_ref, gain_ref, qgain_ref, kgain_ref, cos_ref, sin_ref, base_ref, p0, p1, p2, p3, w0, w1, w2, w3,
    stream_out, partial_out, projected_out, probs_out, att_out,
):
    bits = bits_ref[0]
    weights = (w0, w1, w2, w3)
    stream = plus_parts(base_ref, (p0, p1, p2, p3))
    stream_out[...] = stream
    normed = (stream * scaling_of(stream) * gain_ref[...]).astype(BF)
    projected = jnp.zeros((128, 512), F32)
    for part, weight in zip(kernel_order(cut_blocks(normed), bits), weights):
        projected += dot(part, weight[:, :512])
    projected_out[...] = projected
    cosine, sine = cos_ref[...], sin_ref[...]
    query = heads_turned(projected[:, :256], qgain_ref[...], cosine, sine)[2].astype(BF)
    keys = heads_turned(projected[:, 256:384], kgain_ref[...], cosine[:, :128], sine[:, :128])[2]
    keys = both_places(keys)
    values = both_places(projected[:, 384:])
    causal = rows_of(probs_out[:, :128]) >= lanes_of(probs_out[:, :128])
    for kv in range(2):
        block = query[:, kv * 128 : (kv + 1) * 128]
        mixed = []
        for at in range(2):
            scores = contract_cols(one_head(block, at), keys[at ^ kv]) * HD ** (-0.5)
            scores = jnp.where(causal, scores, MASKED)
            peak = jnp.max(scores, axis=1, keepdims=True)
            logsum = peak + jnp.log(jnp.sum(jnp.exp(scores - peak), axis=1, keepdims=True))
            probs = jnp.exp(scores - logsum)
            head = kv * 2 + at
            probs_out[:, head * 128 : (head + 1) * 128] = probs
            mixed.append(dot(probs.astype(BF), values[at ^ kv]))
        att_out[:, kv * 128 : (kv + 1) * 128] = side_by_side(*mixed).astype(BF)
    att = att_out[...]
    outs = [dot(att, weight[:, 512:]) for weight in weights]
    store_blocks(partial_out, kernel_order(outs, bits))


def attend_backward_kernel(
    bits_ref, gain_ref, qgain_ref, kgain_ref, cos_ref, sin_ref, stream_ref, base_ref, p0, p1, p2, p3,
    projected_ref, probs_ref, att_ref, w0, w1, w2, w3,
    total_out, facing_out, near_out, own_out, back_out, gain_out, qgain_out, kgain_out,
):
    bits = bits_ref[0]
    weights = (w0, w1, w2, w3)
    total = plus_parts(base_ref, (p0, p1, p2, p3))
    total_out[...] = total
    cs = kernel_order(cut_blocks(total.astype(BF)), bits)
    grad = jnp.zeros((128, 256), F32)
    for part, weight in zip(cs, weights):
        grad += contract_cols(part, weight[:, 512:])
    grad = grad.astype(BF)
    cosine, sine = cos_ref[...], sin_ref[...]
    projected = projected_ref[...]
    qnormed, qscaling, query = heads_turned(projected[:, :256], qgain_ref[...], cosine, sine)
    query = query.astype(BF)
    knormed, kscaling, keys = heads_turned(
        projected[:, 256:384], kgain_ref[...], cosine[:, :128], sine[:, :128]
    )
    keys = both_places(keys)
    values = both_places(projected[:, 384:])
    dquery, dkeys, dvalues = [], [], []
    for kv in range(2):
        block = query[:, kv * 128 : (kv + 1) * 128]
        gblock = grad[:, kv * 128 : (kv + 1) * 128]
        dqs = []
        dk = jnp.zeros((128, 128), F32)
        dv = jnp.zeros((128, 128), F32)
        for at in range(2):
            head = kv * 2 + at
            probs = probs_ref[:, head * 128 : (head + 1) * 128]
            mine = one_head(gblock, at)
            dv += dot(probs.T.astype(BF), mine)
            dprobs = contract_cols(mine, values[at ^ kv])
            delta = jnp.sum(probs * dprobs, axis=1, keepdims=True)
            dscores = probs * (dprobs - delta)
            dqs.append(dot(dscores.astype(BF), keys[at ^ kv]))
            dk += dot(dscores.T.astype(BF), one_head(block, at))
        dquery.append(side_by_side(*dqs) * HD ** (-0.5))
        dkeys.append((dk + pltpu.roll(dk, HD, 1)) * HD ** (-0.5))
        dvalues.append(dv + pltpu.roll(dv, HD, 1))
    dquery = jnp.concatenate(dquery, axis=1)
    dquery, qgain = heads_back(dquery, qnormed, qscaling, qgain_ref[...], cosine, sine)
    dkeys, kgain = heads_back(
        side_by_side(*dkeys), knormed, kscaling, kgain_ref[...], cosine[:, :128], sine[:, :128]
    )
    qgain_out[...] = qgain
    kgain_out[...] = kgain
    pieces = jnp.concatenate([dquery, dkeys, side_by_side(*dvalues)], axis=1).astype(BF)
    outs = [contract_cols(pieces, weight[:, :512]) for weight in weights]
    grad = jnp.concatenate(kernel_order(outs, bits), axis=1)
    stream = stream_ref[...]
    back_out[...] = norm_grad(stream, grad, gain_ref[...], gain_out).astype(BF)
    normed = (stream * scaling_of(stream) * gain_ref[...]).astype(BF)
    ns = kernel_order(cut_blocks(normed), bits)
    store_bundles(ns, cs, [pieces, att_ref[...]], facing_out, near_out, own_out)


def shifted_down(x, count):
    if count == 0:
        return x
    return jnp.where(rows_of(x) >= count, pltpu.roll(x, count, 0), 0.0)


def shifted_up(x, count):
    if count == 0:
        return x
    rows = x.shape[0]
    return jnp.where(rows_of(x) < rows - count, pltpu.roll(x, rows - count, 0), 0.0)


def mixer_weights(own_in, core_in, low, high, core_low, core_high, own_out, core_out):
    ins = [
        [own_in[k], core_in[k], (low, high)[k // 2][k % 2], (core_low, core_high)[k // 2][k % 2]]
        for k in range(3)
    ]
    return ins, [own_out[...], core_out[...], high[1], core_high[1]]


def convolved(bx, taps_ref):
    return sum(shifted_down(bx, KW - 1 - k) * taps_ref[k : k + 1, :] for k in range(KW))


def mixer_forward_kernel(bits_ref, gain_ref, taps_ref, stream_ref, *refs):
    ins, outs = mixer_weights(*refs[:8])
    partial_out, projected_out, mix_out = refs[8:]
    bits = bits_ref[0]
    stream = stream_ref[...]
    normed = (stream * scaling_of(stream) * gain_ref[...]).astype(BF)
    ns = kernel_order(cut_blocks(normed), bits)
    projected = []
    for k in range(3):
        total = jnp.zeros((128, 256), F32)
        for part, weight in zip(ns, ins[k]):
            total += dot(part, weight)
        projected.append(total)
        projected_out[k] = total
    mix = (projected[1] * convolved(projected[0] * projected[2], taps_ref)).astype(BF)
    mix_out[...] = mix
    store_blocks(partial_out, kernel_order([dot(mix, weight) for weight in outs], bits))


def mixer_backward_kernel(
    bits_ref, gain_ref, taps_ref, stream_ref, base_ref, p0, p1, p2, p3, start_ref, projected_ref, mix_ref, *refs
):
    ins, outs = mixer_weights(*refs[:8])
    facing_out, near_out, own_out, back_out, gain_out, taps_out = refs[8:]
    bits = bits_ref[0]
    total = plus_parts(base_ref, (p0, p1, p2, p3))
    cs = kernel_order(cut_blocks(total.astype(BF)), bits)
    dmix = jnp.zeros((128, 256), F32)
    for part, weight in zip(cs, outs):
        dmix += contract_cols(part, weight)
    pb, pc, px = projected_ref[0], projected_ref[1], projected_ref[2]
    bx = pb * px
    dconv = dmix * pc
    for k in range(KW):
        taps_out[k : k + 1, :] = jnp.sum(
            dconv * shifted_down(bx, KW - 1 - k), axis=0, keepdims=True
        )
    dbx = sum(shifted_up(dconv, KW - 1 - k) * taps_ref[k : k + 1, :] for k in range(KW))
    pieces = [
        (dbx * px).astype(BF),
        (dmix * convolved(bx, taps_ref)).astype(BF),
        (dbx * pb).astype(BF),
    ]
    grads = []
    for i in range(4):
        grads.append(sum(contract_cols(pieces[k], ins[k][i]) for k in range(3)))
    grad = jnp.concatenate(kernel_order(grads, bits), axis=1)
    stream = stream_ref[...]
    back = norm_grad(stream, grad, gain_ref[...], gain_out) + 0.25 * (total - start_ref[...])
    store_blocks(back_out, kernel_order(cut_blocks(back.astype(BF)), bits_ref[1]))
    normed = (stream * scaling_of(stream) * gain_ref[...]).astype(BF)
    ns = kernel_order(cut_blocks(normed), bits)
    store_bundles(ns, cs, pieces + [mix_ref[...]], facing_out, near_out, own_out)


def in_one_step(kernel, args, outs, flops):
    return pl.pallas_call(
        kernel,
        grid=(1,),
        in_specs=[pl.BlockSpec(memory_space=pltpu.SMEM)] + [whole(x.shape) for x in args[1:]],
        out_shape=[jax.ShapeDtypeStruct(shape, dtype) for shape, dtype in outs],
        out_specs=[whole(shape) for shape, dtype in outs],
        compiler_params=pltpu.CompilerParams(vmem_limit_bytes=VMEM),
        cost_estimate=pl.CostEstimate(
            flops=flops, bytes_accessed=6 * 2**20, transcendentals=128 * 1024
        ),
    )(*args)


def tied(*values):
    return lax.optimization_barrier(values)


def unpack_kernel(in_ref, upper_out, lower_out):
    for k in range(2):
        for i in range(9):
            at = (k * 9 + i) * 256
            upper_out[k, :, i * 128 : (i + 1) * 128] = in_ref[at : at + 256, :].astype(F32)
    for i in range(3):
        for half in range(2):
            at = 18 * 256 + (i * 2 + half) * TILE
            lower_out[i * TILE : (i + 1) * TILE, half * 128 : (half + 1) * 128] = in_ref[
                at : at + TILE, :
            ].astype(F32)


def ffn_unpacked(grads):
    shapes = [(2, 256, 3 * TILE), (3 * TILE, 256)]
    return pl.pallas_call(
        unpack_kernel,
        grid=(1,),
        in_specs=[whole(grads.shape)],
        out_shape=[jax.ShapeDtypeStruct(shape, F32) for shape in shapes],
        out_specs=[whole(shape) for shape in shapes],
        compiler_params=pltpu.CompilerParams(vmem_limit_bytes=VMEM),
    )(grads)


def scattered_z(g):
    return lax.psum_scatter(g, "z", scatter_dimension=0, tiled=True)


def plus_xl(part):
    return (part.astype(F32) + from_xl(part).astype(F32)).astype(BF)


def gathered_z_directly(piece):
    pieces = [piece] + [from_z(piece, bits) for bits in (1, 2, 3)]
    return jnp.concatenate(xor_order(pieces, lax.axis_index("z")), axis=0)


def gathered_z(part):
    return lax.all_gather(part, "z", axis=0, tiled=True)


def body(
    stream_in,
    cotangent,
    mixer_gain,
    mixer_input,
    mixer_kernel,
    mixer_output,
    front_gain,
    front_upper,
    front_lower,
    attend_gain,
    attend_query,
    attend_keyval,
    query_gain,
    key_gain,
    attend_output,
    rear_gain,
    rear_upper,
    rear_lower,
):
    bits = place()[0].astype(jnp.int32).reshape(1)
    x, cot = spread_in([stream_in, cotangent])
    even = lax.axis_index("xl") == 0
    mixer_got = from_facing(
        jnp.where(
            even,
            mixer_input[:2],
            jnp.concatenate([mixer_input[2:], mixer_output[None]], axis=0),
        )
    )
    x, mixer_got, gains, front_upper, front_lower = tied(
        x,
        mixer_got,
        jnp.stack([mixer_gain, front_gain, attend_gain, rear_gain]),
        front_upper,
        front_lower,
    )
    gains = whole_order(gathered(gains))
    mixer_other = from_xl(mixer_got)
    fu = front_upper
    fu_got = facing_half(fu)
    fl_facing = from_facing(front_lower)
    low = jnp.where(even, mixer_other, mixer_got)
    high = jnp.where(even, mixer_got, mixer_other)
    core_input, core_output = from_core(mixer_input), from_core(mixer_output)
    core_low, core_high = from_core(low), from_core(high)
    mixer = [mixer_input, core_input, low, high, core_low, core_high, mixer_output, core_output]
    attend = jnp.concatenate(
        [attend_query, attend_keyval[0], attend_keyval[1], attend_output], axis=1
    )
    tokens, width = x.shape
    wide = (tokens, width)
    cosine, sine = rope_tables(tokens)
    tables = [
        gains[2:3],
        jnp.tile(query_gain, 4)[None],
        jnp.tile(key_gain, 2)[None],
        jnp.tile(cosine[:, 0], (1, 4)),
        jnp.tile(sine[:, 0], (1, 4)),
    ]
    partial, projected, mixes = in_one_step(
        mixer_forward_kernel,
        [bits, gains[:1], mixer_kernel, x] + mixer,
        [(wide, BF), ((3, tokens, 256), F32), ((tokens, 256), BF)],
        2 * tokens * width * 1024,
    )
    partial, fu_got = tied(partial, fu_got)
    parts = over_y(partial)
    fu_other = from_xl(fu_got)
    parts, fu_other, fl_facing, attend = tied(parts, fu_other, fl_facing, attend)
    attend_facing = from_facing(attend)
    fu = with_facing(fu, fu_got, fu_other)
    fl = [front_lower, from_core(front_lower), fl_facing, from_core(fl_facing)]
    first, partial, *front_saved = ffn(
        True, False, bits, gains[1:2], x, parts, None, None, None, fu, fl
    )
    partial, attend_facing, rear_upper = tied(partial, attend_facing, rear_upper)
    attend = [attend, from_core(attend), attend_facing, from_core(attend_facing)]
    ru = gathered_apart(rear_upper)
    parts, rear_lower = tied(over_y(partial), rear_lower)
    rl_facing = from_facing(rear_lower)
    second, partial, attn_projected, probs, attended = in_one_step(
        attend_forward_kernel,
        [bits] + tables + [first] + parts + attend,
        [
            (wide, F32),
            (wide, BF),
            ((tokens, 512), F32),
            ((tokens, 512), F32),
            ((tokens, 256), BF),
        ],
        2 * tokens * width * 1024,
    )
    parts, rl_facing = tied(over_y(partial), rl_facing)
    rl = [rear_lower, from_core(rear_lower), rl_facing, from_core(rl_facing)]
    third, partial, facing_bundle, near_bundle, own, back, rear_gain_grad = ffn(
        True, True, bits, gains[3:4], second, parts, cot, None, None, ru, rl
    )
    sent_out = jnp.concatenate(
        xor_order(blocks((partial.astype(F32) + 0.25 * (third - x)).astype(BF)), place()[1]), axis=1
    )
    rear_near = from_core(near_bundle)
    back_parts, facing_bundle = tied(over_y(back), facing_bundle)
    rear_facing = from_facing(facing_bundle)
    rear_mine, rear_own = near_bundle, own
    (
        third_grad,
        attn_facing,
        attn_mine,
        attn_own,
        sent,
        attend_gain_grad,
        qgain_grad,
        kgain_grad,
    ) = in_one_step(
        attend_backward_kernel,
        [bits] + tables + [second, cot] + back_parts + [attn_projected, probs, attended] + attend,
        [
            (wide, F32),
            ((tokens, 1792), BF),
            ((tokens, 1280), BF),
            ((tokens, 512), BF),
            (wide, BF),
            ((1, width), F32),
            ((1, 256), F32),
            ((1, 128), F32),
        ],
        4 * tokens * width * 1024,
    )
    qgain_grad = jnp.sum(qgain_grad.reshape(4, HD), axis=0)
    kgain_grad = jnp.sum(kgain_grad.reshape(2, HD), axis=0)
    parts, rear_facing, rear_near, attn_facing, attn_mine = tied(
        over_y(sent), rear_facing, rear_near, attn_facing, attn_mine
    )
    attn_facing = from_facing(attn_facing)
    rear_far = from_core(rear_facing)
    second_grad, facing_bundle, near_bundle, own, back, front_gain_grad = ffn(
        False, True, bits, gains[1:2], first, None, third_grad, parts, front_saved, fu, fl
    )
    back, attn_facing = tied(back, attn_facing)
    parts = over_y(back)
    front_facing = from_facing(facing_bundle)
    parts[1], rear_far = tied(parts[1], rear_far)
    rear_grads = weight_grads(TILE, 6, rear_own, rear_mine, rear_near, rear_facing, rear_far)
    rear_part = scattered_z(rear_grads)
    parts, rear_grads, near_bundle, attn_mine = tied(parts, rear_grads, near_bundle, attn_mine)
    front_near = from_core(near_bundle)
    attn_near = from_core(attn_mine)
    mixer_facing, mixer_mine, mixer_own, stream_back, mixer_gain_grad, kernel_grad = in_one_step(
        mixer_backward_kernel,
        [jnp.stack(place()).astype(jnp.int32), gains[:1], mixer_kernel, x, second_grad]
        + parts
        + [cot, projected, mixes]
        + mixer,
        [
            ((tokens, 2048), BF),
            ((tokens, 1536), BF),
            ((tokens, 512), BF),
            (wide, BF),
            ((1, width), F32),
            ((KW, 256), F32),
        ],
        4 * tokens * width * 1024,
    )
    own, stream_back, mixer_facing, mixer_mine, rear_part = tied(
        own, stream_back, mixer_facing, mixer_mine, rear_part
    )
    mixer_near = from_core(mixer_mine)
    mixer_facing = from_facing(mixer_facing)
    rear_part = plus_xl(rear_part)
    gain_rows = jnp.concatenate(
        [mixer_gain_grad, front_gain_grad, attend_gain_grad, rear_gain_grad], axis=0
    )
    head_row = jnp.pad(jnp.concatenate([qgain_grad, kgain_grad]), (0, width - 2 * HD))[None]
    rows = jnp.concatenate([gain_rows, head_row], axis=0)
    rows = rows + from_y(rows, 1) + from_y(rows, 2) + from_y(rows, 3)
    own_row, near_row, far_row, last_row = own_order(rows[:4])
    others = jnp.concatenate([kernel_grad, rows[4:, :256]], axis=0)
    got = from_core(jnp.concatenate([near_row, last_row, others], axis=0))
    rows = jnp.concatenate([own_row, far_row, others], axis=0) + got
    rows = jnp.concatenate([rows[:4], rows[8:]], axis=0) + from_facing(rows[4:])
    rows = jnp.pad(jnp.concatenate([rows[:, :128], rows[:, 128:]], axis=0), ((0, 48), (0, 0)))

    front_grads = weight_grads(
        TILE, 6, own, near_bundle, front_near, front_facing, from_core(front_facing)
    )
    front_part = scattered_z(front_grads)
    front_grads, mixer_facing, rear_part = tied(front_grads, mixer_facing, rear_part)
    attn_grads = weight_grads(
        256, 2, attn_own, attn_mine, attn_near, attn_facing, from_core(attn_facing)
    )
    mixer_grads = weight_grads(
        256, 3, mixer_own, mixer_mine, mixer_near, mixer_facing, from_core(mixer_facing)
    )
    rear_all = gathered_z(rear_part)
    bundle, front_part = tied(
        jnp.concatenate([mixer_grads, attn_grads, rows.astype(BF)], axis=0), front_part
    )
    front_part = plus_xl(front_part)
    sent = dp_sum_begun(bundle)
    sent, front_part, stream_back, sent_out = tied(sent, front_part, stream_back, sent_out)
    sum_back, sum_out = bring_back([stream_back, sent_out])
    stream_grad = cotangent + sum_back
    fourth = stream_in + sum_out
    small_grads = dp_sum_ended(sent)
    front_all = gathered_z(front_part)
    rear_upper_grad, rear_lower_grad = ffn_unpacked(rear_all)
    rear_upper_grad, rear_lower_grad, small_grads, stream_grad, fourth, front_all = tied(
        rear_upper_grad, rear_lower_grad, small_grads, stream_grad, fourth, front_all
    )
    cut = mixer_grads.shape[0]
    mixer_grads, attn_grads = small_grads[:cut], small_grads[cut : cut + attn_grads.shape[0]]
    rows = small_grads[-64:-48].astype(F32)
    sums = jnp.concatenate([rows[:8], rows[8:]], axis=1)
    input_grad = jnp.stack([unpacked(mixer_grads, 256, 1, k) for k in range(3)])
    mixer_output_grad = unpacked_lower(mixer_grads, 256, 3)
    attend_query_grad = unpacked(attn_grads, 256, 1, 0)
    keyval_grad = attn_grads[512:1024].astype(F32).reshape(2, 256, 128)
    attend_output_grad = unpacked_lower(attn_grads, 256, 2)
    front_upper_grad, front_lower_grad = ffn_unpacked(front_all)
    return (
        fourth,
        stream_grad,
        sums[0],
        input_grad,
        sums[4:7],
        mixer_output_grad,
        sums[1],
        front_upper_grad,
        front_lower_grad,
        sums[2],
        attend_query_grad,
        keyval_grad,
        sums[7, :HD],
        sums[7, HD : 2 * HD],
        attend_output_grad,
        sums[3],
        rear_upper_grad,
        rear_lower_grad,
    )


def solution(mesh):
    parts = Mesh(mesh.devices.reshape(4, 2, 2, 2, 4), ("z", "xl", "xh", "core", "y"))
    tokens = ("z", "xl", "y")
    row = ("xh", "core")
    stream = P(tokens, row)
    gain = P(row)
    upper = P(None, row, "y")
    lower = P("y", row)
    weights = (
        gain,
        upper,
        P(None, "y"),
        lower,
        gain,
        upper,
        lower,
        gain,
        P(row, "y"),
        upper,
        P(),
        P(),
        lower,
        gain,
        upper,
        lower,
    )
    return jax.shard_map(
        body,
        mesh=parts,
        in_specs=(stream, stream) + weights,
        out_specs=(stream, stream) + weights,
        check_vma=False,
    )
```
